32 devices in a mesh: lat: 2 (over core), lev: 16 (over z, y, x).
Axes of the slice: x: 2, y: 2, z: 4, core: 2. Of those that a mesh axis runs over, the one named last changes fastest.
Arguments:
- field: float32 [32, 8, 128, 1152], P('lev', None, 'lat'), may hold values from 0.05 to 5
- courant: float32 [3, 32, 128, 1152], P(None, 'lev', 'lat'), may hold values from 0.02 to 0.3
- parcel_mass: float32 [8, 131072], P(None, ('lat', 'lev')), may hold values from 0.5 to 20
- parcel_owner: int32 [131072, 1], P(('lat', 'lev')), may hold values from 0 to 31; in each aligned block of 4096 rows (0 to 4095, 4096 to 8191, ...) at most 256 rows name the same one
- parcel_cell: int32 [131072], P(('lat', 'lev')), may hold values from 0 to 147455
- settle: float32 [8, 32], replicated, may hold values from 0.3 to 8
- coag_gain: float32 [8, 8, 8], replicated, may hold values from 0.002 to 0.03
- coag_loss: float32 [8, 8], replicated, may hold values from 0.02 to 0.5
Outputs:
- result: float32 [32, 8, 128, 1152], P('lev', None, 'lat')
The draws below stay inside these ranges and needn't reach their ends.
Inputs may be any that keep to these rules, and one draw needn't show every extreme that they name: `parcel_owner`: among the parcels of one device, at most 256 have the same owner, and in some devices exactly 256 do.
All inputs are finite; a program needn't handle non-finite values.
Results may differ from the reference program's by a relative error of at most 0.0003.
Values sent between devices are 32-bit elements; how exact they have to be, the bound alone decides.
No kernel may reach another device: no remote copies, remote signals or barrier semaphores. Data moves between devices by JAX's collectives and lax.ppermute only.
A program may use at most 192 MiB of HBM per device.

```python
import math
import jax
import jax.numpy as jnp
import numpy as np
from jax import lax

B = 8
NX = 1152
LAT_DEV = 64
LEV_DEV = 2
PARCELS_DEV = 4096
ADV_STEPS = 2
NY = 128
NZ = 32
PARCELS = 131072
CAP = 256
CELLS_DEV = 147456
N_LAT = 2
N_LEV = 16
DEVICES = 32


def place_ends(entries, rng, smallest, largest):
    spot = [jax.random.randint(jax.random.fold_in(rng, axis), (), 0, length) for axis, length in enumerate(entries.shape)]
    widest = entries.shape.index(max(entries.shape))
    beside = spot[:widest] + [(spot[widest] + 1) % entries.shape[widest]] + spot[widest + 1:]
    return entries.at[tuple(spot)].set(smallest).at[tuple(beside)].set(largest)


def steps_of(stream_key, extent, shards, low, top_value):
    def one(axis_at, shards_of):
        heights = jax.random.uniform(jax.random.fold_in(jax.random.fold_in(stream_key, 6), axis_at), (shards_of,), jnp.float32, low / len(shards), top_value / len(shards))
        return jnp.repeat(jnp.exp(heights), extent[axis_at] // shards_of).reshape((-1,) + (1,) * (len(extent) - axis_at - 1))

    gain = one(*shards[0])
    for cut in shards[1:]:
        gain = gain * one(*cut)
    return gain


def routed_block(own_key, own, number, rows, number_of, top, most, skew):
    ranking = jax.random.permutation(own_key, number_of)
    packed, usual = portions_of(number_of, rows * top, most, skew, True), portions_of(number_of, rows * top, most, skew, False)
    places = jnp.arange(number_of)

    def named(sizes, rotation):
        used = int((sizes > 0).sum())
        fixed = max(1, used // 4)
        moved = fixed + (places - fixed + rotation * (used - fixed)) % max(1, number_of - fixed)
        return jnp.zeros((number_of,), jnp.int32).at[ranking[jnp.where(places < fixed, places, moved)]].set(jnp.asarray(sizes, jnp.int32))

    sizes = jnp.where(number % 4 == 0, named(packed, number // 4), named(usual, number - number // 4 - 1))
    mixed = jax.random.permutation(jax.random.fold_in(own, 3), number_of)
    donor, receiver = mixed[0:number_of // 2 * 2:2], mixed[1:number_of // 2 * 2:2]
    slack = jnp.minimum(sizes[donor] - 1, most - sizes[receiver]) // 2
    slack = jnp.where((donor == ranking[0]) | (receiver == ranking[0]) | (sizes[receiver] == 0), 0, jnp.maximum(slack, 0))
    moved = jax.random.randint(jax.random.fold_in(own, 4), (number_of // 2,), 0, 1 << 20) % (slack + 1)
    sizes = sizes.at[donor].add(-moved).at[receiver].add(moved)
    labels = jnp.searchsorted(jnp.cumsum(sizes), jnp.arange(rows * top), side="right").astype(jnp.int32)
    grid = labels.reshape(top, rows).T
    grid = grid[jax.random.permutation(jax.random.fold_in(own, 1), rows)]
    rotation = jax.random.randint(jax.random.fold_in(own, 2), (rows, 1), 0, top)
    return jnp.take_along_axis(grid, (jnp.arange(top)[None, :] + rotation) % top, axis=1)


def portions_of(amount, total, reach, skew, full):
    portions = [(1 << 20) // math.isqrt(grade ** skew) + 1 for grade in range(1, amount + 1)]
    largest = reach if full else min(reach, max(-(-total // amount), total * portions[0] // sum(portions)))
    least = 1 if total - largest >= amount - 1 else 0
    holding, surplus = [largest] + [least] * (amount - 1), total - largest - least * (amount - 1)
    while surplus > 0:
        movable = [i for i in range(1, amount) if holding[i] < largest] or [i for i in range(1, amount) if holding[i] < reach]
        mass, left = sum([portions[i] for i in movable]), surplus
        for i in movable:
            extra = min(reach - holding[i], max(1, left * portions[i] // mass), surplus)
            holding[i] = holding[i] + extra
            surplus = surplus - extra
    return np.array(holding)


def setup_inputs(seed: int = 0) -> dict:
    key_of = jax.random.split(jax.random.key(seed), 9)
    field = jnp.clip(jnp.exp(math.log(5.0) - 4.6051702 * jax.random.uniform(key_of[0], (NZ, B, NY, NX), jnp.float32) ** steps_of(key_of[0], (NZ, B, NY, NX), ((0, 16), (2, 2)), -0.2, 0.2)), 0.05, 5.0)
    courant = jnp.clip(0.02 + 0.28 * jax.random.uniform(key_of[1], (3, NZ, NY, NX), jnp.float32) ** steps_of(key_of[1], (3, NZ, NY, NX), ((1, 16), (2, 2)), -0.2, 0.2), 0.02, 0.3)
    parcel_mass = jnp.clip(jnp.exp(math.log(20.0) - 3.6888795 * jax.random.uniform(key_of[2], (B, PARCELS), jnp.float32) ** steps_of(key_of[2], (B, PARCELS), ((1, 32),), -0.2, 0.2)), 0.5, 20.0)
    parcel_owner_keys = jax.random.split(jax.random.fold_in(key_of[3], 1), PARCELS // PARCELS_DEV)
    parcel_owner_turns = jax.random.permutation(jax.random.fold_in(key_of[3], 3), PARCELS // PARCELS_DEV)
    parcel_owner = jax.vmap(lambda own, number: routed_block(jax.random.fold_in(key_of[3], 2), own, number, PARCELS_DEV, DEVICES, 1, CAP, 2))(parcel_owner_keys, parcel_owner_turns).reshape((PARCELS, 1))
    parcel_cell = place_ends(jax.random.randint(key_of[4], (PARCELS,), 0, CELLS_DEV), jax.random.fold_in(key_of[4], 1), 0, CELLS_DEV - 1).astype(jnp.int32)
    settle = jnp.clip(jnp.exp(jax.random.uniform(key_of[5], (B, NZ), jnp.float32, math.log(0.3), math.log(8.0))), 0.3, 8.0)
    coag_gain = jnp.clip(jnp.exp(jax.random.uniform(key_of[6], (B, B, B), jnp.float32, math.log(0.002), math.log(0.03))), 0.002, 0.03)
    coag_loss = jnp.clip(jnp.exp(jax.random.uniform(key_of[7], (B, B), jnp.float32, math.log(0.02), math.log(0.5))), 0.02, 0.5)
    return dict(field=field, courant=courant, parcel_mass=parcel_mass, parcel_owner=parcel_owner, parcel_cell=parcel_cell, settle=settle, coag_gain=coag_gain, coag_loss=coag_loss)


def column_physics(columns, settle, coag_gain, coag_loss):
    bin_count = columns.shape[1]
    lower_coeff = jnp.concatenate([jnp.zeros_like(settle[:, :1]), settle[:, :-1]], axis=1)
    gain_matrix = coag_gain.reshape(bin_count * bin_count, bin_count)

    def advance_level(carry, inputs):
        forcing, upper_coeff, diag_coeff = inputs
        solved = (forcing + upper_coeff[:, None] * carry) / (1.0 + diag_coeff[:, None])
        loss_rate = jnp.dot(coag_loss, solved, precision=lax.Precision.HIGHEST, preferred_element_type=jnp.float32)
        inner = jnp.dot(gain_matrix, solved, precision=lax.Precision.HIGHEST, preferred_element_type=jnp.float32)
        gain_terms = jnp.sum(inner.reshape(bin_count, bin_count, -1) * solved[None, :, :], axis=1)
        return solved, (solved + gain_terms) / (1.0 + loss_rate)

    initial = jnp.zeros_like(columns[0])
    unused, treated = lax.scan(advance_level, initial, (columns, lower_coeff.T, settle.T))
    return treated


def reference(field, courant, parcel_mass, parcel_owner, parcel_cell, settle, coag_gain, coag_loss):
    bin_count = field.shape[1]
    cell_count = LAT_DEV * LEV_DEV * NX
    blocks = field.reshape(N_LEV, LEV_DEV, bin_count, N_LAT, LAT_DEV, NX).transpose(2, 3, 0, 1, 4, 5).reshape(bin_count, N_LAT * N_LEV * cell_count)
    target = (parcel_owner[:, 0] * cell_count + parcel_cell).astype(jnp.int32)
    blocks = blocks.at[:, target].add(parcel_mass)
    field = blocks.reshape(bin_count, N_LAT, N_LEV, LEV_DEV, LAT_DEV, NX).transpose(2, 3, 0, 1, 4, 5).reshape(NZ, bin_count, NY, NX)
    for repeat in range(ADV_STEPS):
        west_cells = jnp.roll(field, 1, axis=3)
        south_cells = jnp.pad(field, ((0, 0), (0, 0), (1, 0), (0, 0)))[:, :, :-1]
        above_cells = jnp.pad(field, ((1, 0), (0, 0), (0, 0), (0, 0)))[:-1]
        field = field - courant[0][:, None] * (field - west_cells) - courant[1][:, None] * (field - south_cells) - courant[2][:, None] * (field - above_cells)
    treated = column_physics(field.reshape(NZ, bin_count, NY * NX), settle, coag_gain, coag_loss)
    return treated.reshape(NZ, bin_count, NY, NX)
```

```python
import functools

import jax
import jax.numpy as jnp
from jax import lax
from jax.experimental import pallas as pl
from jax.experimental.pallas import tpu as pltpu
from jax.sharding import PartitionSpec as P

ADV_STEPS = 2
LANES = 128
ROUTE_BLOCK = 256
ACCS = 4
UNROLL = 8
VMEM = pl.BlockSpec(memory_space=pltpu.VMEM)
SMEM = pl.BlockSpec(memory_space=pltpu.SMEM)
BIG = pltpu.CompilerParams(vmem_limit_bytes=56 * 1024 * 1024)


def route_kernel(devices, cap_lanes, level_cells, owner_ref, cell_ref, mass_ref, out_ref, a_ref, c_ref, b_ref):
    parcels = owner_ref.shape[1]
    blocks = cap_lanes // LANES
    width = ROUTE_BLOCK
    dev_ids = lax.broadcasted_iota(jnp.int32, (devices, width), 0)
    before = (
        lax.broadcasted_iota(jnp.int32, (width, width), 0) < lax.broadcasted_iota(jnp.int32, (width, width), 1)
    ).astype(jnp.bfloat16)
    slot_ids = lax.broadcasted_iota(jnp.int32, (cap_lanes, width), 0)

    def masks(start):
        owner = owner_ref[:, pl.ds(start, width)]
        cell = cell_ref[:, pl.ds(start, width)]
        mine = owner == dev_ids
        low = cell >= level_cells
        return owner, cell, jnp.where(mine & low, 1.0, 0.0), jnp.where(mine & (~low), 1.0, 0.0)

    low_total = jnp.zeros((devices, 1), jnp.float32)
    for start in range(0, parcels, width):
        unused, unused, low, high = masks(start)
        low_total = low_total + jnp.sum(low, axis=1, keepdims=True)
    low_base = jnp.zeros((devices, 1), jnp.float32)
    high_base = low_total
    for start in range(0, parcels, width):
        owner, cell, low, high = masks(start)
        both = jnp.concatenate([low, high], axis=0)
        earlier = jnp.dot(both.astype(jnp.bfloat16), before, preferred_element_type=jnp.float32)
        rank = jnp.sum(both * (earlier + jnp.concatenate([low_base, high_base], axis=0)), axis=0, keepdims=True)
        low_base = low_base + jnp.sum(low, axis=1, keepdims=True)
        high_base = high_base + jnp.sum(high, axis=1, keepdims=True)
        b_ref[:, pl.ds(start, width)] = jnp.where(slot_ids == rank.astype(jnp.int32), 1.0, 0.0).astype(jnp.bfloat16)
        mass = mass_ref[:, pl.ds(start, width)]
        coarse = mass.astype(jnp.bfloat16).astype(jnp.float32)
        fine = mass - coarse
        owner_rows = jnp.broadcast_to(owner, (8, width))
        for device in range(0, devices, 2):
            for part, piece in enumerate((coarse, fine)):
                pair = jnp.concatenate(
                    [jnp.where(owner_rows == device + extra, piece, 0.0) for extra in range(2)], axis=0
                )
                a_ref[pl.ds(part * devices * 8 + device * 8, 16), pl.ds(start, width)] = pair.astype(jnp.bfloat16)
        mine = low + high
        for part, piece in enumerate((cell >> 16, (cell >> 8) & 255, cell & 255)):
            c_ref[pl.ds(part * devices, devices), pl.ds(start, width)] = (mine * piece.astype(jnp.float32)).astype(
                jnp.bfloat16
            )
    contract = (((1,), (1,)), ((), ()))
    sorted_mass = lax.dot_general(a_ref[...], b_ref[...], contract, preferred_element_type=jnp.float32)
    sorted_cell = lax.dot_general(c_ref[...], b_ref[...], contract, preferred_element_type=jnp.float32)
    code = (
        sorted_cell[:devices] * 65536.0 + sorted_cell[devices : 2 * devices] * 256.0 + sorted_cell[2 * devices :]
    )
    total = sorted_mass[: devices * 8] + sorted_mass[devices * 8 :]
    out_ref[:, :, pl.ds(0, cap_lanes)] = total.reshape(devices, 8, cap_lanes)
    rows = lax.broadcasted_iota(jnp.int32, (8, LANES), 0)
    for device in range(devices):
        tile = jnp.zeros((8, LANES), jnp.float32)
        for block in range(blocks):
            tile = jnp.where(rows == block, code[device : device + 1, block * LANES : (block + 1) * LANES], tile)
        tile = jnp.where(rows == blocks, high_base[device : device + 1], tile)
        tile = jnp.where(rows == blocks + 1, low_base[device : device + 1], tile)
        out_ref[device, :, pl.ds(cap_lanes, LANES)] = tile


def route(parcel_mass, parcel_owner, parcel_cell, devices, level_cells):
    parcels = parcel_owner.shape[0]
    capacity = 2 * parcels // devices
    cap_lanes = -(-capacity // LANES) * LANES
    return pl.pallas_call(
        functools.partial(route_kernel, devices, cap_lanes, level_cells),
        out_shape=jax.ShapeDtypeStruct((devices, 8, cap_lanes + LANES), jnp.float32),
        in_specs=[VMEM] * 3,
        out_specs=VMEM,
        scratch_shapes=[
            pltpu.VMEM((devices * 16, parcels), jnp.bfloat16),
            pltpu.VMEM((devices * 3, parcels), jnp.bfloat16),
            pltpu.VMEM((cap_lanes, parcels), jnp.bfloat16),
        ],
        compiler_params=BIG,
        name="route",
    )(parcel_owner.reshape(1, parcels), parcel_cell.reshape(1, parcels), parcel_mass)


def deposit_kernel(row_offset, counts_ref, codes_ref, slots_ref, field_ref, out_ref, *accs):
    sources, unused, width = slots_ref.shape
    cap_lanes = width - LANES
    levels, bins, lats, lons = field_ref.shape
    lon_blocks = lons // LANES
    rows = levels * lats * lon_blocks
    lane_ids = lax.broadcasted_iota(jnp.int32, (8, LANES), 1)

    def clear(index, carry):
        for acc in accs:
            acc[pl.ds(index * 8, 8)] = jnp.zeros((8, 8, LANES), jnp.float32)
        return carry

    lax.fori_loop(0, rows // 8, clear, 0)

    def from_source(source, carry):
        def chunk(index, carry):
            first = index * UNROLL
            block = first // LANES
            masses = slots_ref[source, :, pl.ds(pl.multiple_of(block * LANES, LANES), LANES)]
            base = source * cap_lanes + first
            for step in range(UNROLL):
                code = codes_ref[base + step]
                row = (code >> 7) - row_offset
                if row_offset:
                    row = jnp.where(row < 0, rows, row)
                lane = code & (LANES - 1)
                moved = pltpu.roll(masses, (lane - first - step) & (LANES - 1), 1)
                acc = accs[step % ACCS]
                acc[row] = acc[row] + jnp.where(lane_ids == lane, moved, 0.0)
            return carry

        return lax.fori_loop(0, (counts_ref[source] + UNROLL - 1) // UNROLL, chunk, carry)

    lax.fori_loop(0, sources, from_source, 0)

    flat = [acc.reshape((rows + 8) * 8, LANES) for acc in accs]

    def merge(index, carry):
        level = index // (lats // 8)
        lat = (index % (lats // 8)) * 8
        for lon in range(lon_blocks):
            for b in range(bins):
                start = ((level * lats + lat) * lon_blocks + lon) * 8 + b
                picked = pl.ds(start, 8, stride=lon_blocks * 8)
                total = field_ref[level, b, pl.ds(pl.multiple_of(lat, 8), 8), pl.ds(lon * LANES, LANES)]
                for acc in flat:
                    total = total + acc[picked, :]
                out_ref[level, b, pl.ds(pl.multiple_of(lat, 8), 8), pl.ds(lon * LANES, LANES)] = total
        return carry

    lax.fori_loop(0, levels * (lats // 8), merge, 0)


def deposit(field, slots, codes, counts, row_offset, name):
    levels, bins, lats, lons = field.shape
    rows = levels * lats * lons // LANES
    return pl.pallas_call(
        functools.partial(deposit_kernel, row_offset),
        out_shape=jax.ShapeDtypeStruct(field.shape, jnp.float32),
        in_specs=[SMEM, SMEM, VMEM, VMEM],
        out_specs=VMEM,
        scratch_shapes=[pltpu.VMEM((rows + 8, 8, LANES), jnp.float32)] * ACCS,
        compiler_params=BIG,
        name=name,
    )(counts, codes, slots, field)


def advance_kernel(par_ref, f_ref, rim_ref, halo_ref, c_ref, ch_ref, cn_ref, adv_ref, hl_ref, p0, p1):
    step = pl.program_id(0)
    bins = f_ref.shape[1]

    @pl.when(step == 0)
    def halo():
        def one(b, carry):
            above = halo_ref[0, b]
            for level in range(2):
                f = halo_ref[1 + level, b]
                rolled = pltpu.roll(f, 1, 0)
                p0[level, b] = rolled
                new = (
                    f
                    - ch_ref[0, level] * (f - pltpu.roll(f, 1, 1))
                    - ch_ref[1, level] * (f - rolled)
                    - ch_ref[2, level] * (f - above)
                )
                p1[level, b] = pltpu.roll(new, 1, 0)
                above = f
            return carry

        lax.fori_loop(0, bins, one, 0)

    @pl.when(step > 0)
    def main():
        top_row = lax.broadcasted_iota(jnp.int32, f_ref.shape[2:], 0) == 0

        def south(prev, level, b, f):
            rolled = pltpu.roll(f, 1, 0)
            out = jnp.where(top_row, prev[level, b], rolled)
            prev[level, b] = rolled
            return out

        def one(b, carry):
            f0 = f_ref[0, b]
            f1 = f_ref[1, b]
            g0 = (
                f0
                - c_ref[0, 0] * (f0 - pltpu.roll(f0, 1, 1))
                - c_ref[1, 0] * (f0 - south(p0, 0, b, f0))
                - c_ref[2, 0] * (f0 - rim_ref[b])
            )
            g1 = (
                f1
                - c_ref[0, 1] * (f1 - pltpu.roll(f1, 1, 1))
                - c_ref[1, 1] * (f1 - south(p0, 1, b, f1))
                - c_ref[2, 1] * (f1 - f0)
            )
            a0 = (
                g0
                - c_ref[0, 0] * (g0 - pltpu.roll(g0, 1, 1))
                - c_ref[1, 0] * (g0 - south(p1, 0, b, g0))
                - c_ref[2, 0] * g0
            )
            a1 = (
                g1
                - c_ref[0, 1] * (g1 - pltpu.roll(g1, 1, 1))
                - c_ref[1, 1] * (g1 - south(p1, 1, b, g1))
                - c_ref[2, 1] * (g1 - g0)
            )
            adv_ref[0, b] = a0
            adv_ref[1, b] = a1
            low = (a1 + par_ref[b] * (a0 * par_ref[8 + b])) * par_ref[24 + b]
            hl_ref[0, b] = cn_ref[...] * g1 + par_ref[16 + b] * low
            return carry

        lax.fori_loop(0, bins, one, 0)


def advance(params, field, rim, halo, courant, courant_halo, courant_next):
    levels, bins, lats, lons = field.shape
    blocks = lats // 8
    at = lambda step: jnp.maximum(step - 1, 0)
    return pl.pallas_call(
        advance_kernel,
        out_shape=(
            jax.ShapeDtypeStruct(field.shape, jnp.float32),
            jax.ShapeDtypeStruct((blocks, bins, 8, lons), jnp.float32),
        ),
        grid=(blocks + 1,),
        in_specs=[
            SMEM,
            pl.BlockSpec((levels, bins, 8, lons), lambda step: (0, 0, at(step), 0)),
            pl.BlockSpec((bins, 8, lons), lambda step: (0, at(step), 0)),
            pl.BlockSpec((3, bins, 8, lons), lambda step: (0, 0, 0, 0)),
            pl.BlockSpec((3, levels, 8, lons), lambda step: (0, 0, at(step), 0)),
            pl.BlockSpec((3, levels, 8, lons), lambda step: (0, 0, 0, 0)),
            pl.BlockSpec((8, lons), lambda step: (at(step), 0)),
        ],
        out_specs=(
            pl.BlockSpec((levels, bins, 8, lons), lambda step: (0, 0, at(step), 0)),
            pl.BlockSpec((1, bins, 8, lons), lambda step: (at(step), 0, 0, 0)),
        ),
        scratch_shapes=[pltpu.VMEM((levels, bins, 8, lons), jnp.float32)] * 2,
        compiler_params=BIG,
        name="advance",
    )(params, field, rim, halo, courant, courant_halo, courant_next)


def cube_end_kernel(lam_ref, hl_ref, out_ref):
    count, bins = hl_ref.shape[:2]

    def one(b, carry):
        h = hl_ref[0, b]
        for member in range(1, count):
            h = hl_ref[member, b] + lam_ref[member * bins + b] * h
        out_ref[b] = h
        return carry

    lax.fori_loop(0, bins, one, 0)


def cube_scan_kernel(lam_ref, hl_ref, hin_ref, out_ref):
    count, bins = hl_ref.shape[:2]

    def one(b, carry):
        h = hin_ref[b]
        out_ref[0, b] = h
        for member in range(count - 1):
            h = hl_ref[member, b] + lam_ref[member * bins + b] * h
            out_ref[member + 1, b] = h
        return carry

    lax.fori_loop(0, bins, one, 0)


def finish_kernel(par_ref, loss_ref, gain_ref, adv_ref, h_ref, out_ref):
    levels, bins, unused, lons = adv_ref.shape
    width = 3 * LANES

    def part(index, carry):
        at = pl.ds(pl.multiple_of(index * width, LANES), width)
        above = [h_ref[0, b, :, at] for b in range(bins)]
        for level in range(2):
            solved = []
            for b in range(bins):
                s = (adv_ref[level, b, :, at] + above[b]) * par_ref[16 * level + 8 + b]
                solved.append(s)
                above[b] = par_ref[b] * s
            for i in range(bins):
                loss = loss_ref[i * bins] * solved[0]
                for j in range(1, bins):
                    loss = loss + loss_ref[i * bins + j] * solved[j]
                total = solved[i]
                base = i * bins * bins
                for j in range(bins):
                    inner = gain_ref[base + j * bins] * solved[0]
                    for k in range(1, j + 1):
                        inner = inner + gain_ref[base + j * bins + k] * solved[k]
                    total = total + inner * solved[j]
                out_ref[level, i, :, at] = total / (1.0 + loss)
        return carry

    lax.fori_loop(0, lons // width, part, 0)


def finish(params, loss, gain, adv, h):
    levels, bins, lats, lons = adv.shape
    return pl.pallas_call(
        finish_kernel,
        out_shape=jax.ShapeDtypeStruct(adv.shape, jnp.float32),
        grid=(lats // 8,),
        in_specs=[
            SMEM,
            SMEM,
            SMEM,
            pl.BlockSpec((levels, bins, 8, lons), lambda step: (0, 0, step, 0)),
            pl.BlockSpec((1, bins, 8, lons), lambda step: (step, 0, 0, 0)),
        ],
        out_specs=pl.BlockSpec((levels, bins, 8, lons), lambda step: (0, 0, step, 0)),
        compiler_params=BIG,
        name="finish",
    )(params, loss, gain, adv, h)


def shifted(value, axis, steps):
    count = lax.axis_size(axis)
    first, last = (max(0, -steps), min(count, count - steps))
    return lax.ppermute(value, axis, [(source, source + steps) for source in range(first, last)])


def on_device(field, courant, parcel_mass, parcel_owner, parcel_cell, settle, coag_gain, coag_loss):
    levels, bins, lats, lons = field.shape
    n_lev = lax.axis_size("lev")
    devices = lax.axis_size(("lat", "lev"))
    cube = lats // 8
    cubes = n_lev // cube
    here = lax.axis_index("lev")

    raw_rim = shifted(field[-1], "lev", 1)
    courant_next = shifted(courant[2, 0], "lev", -1)
    courant_halo = shifted(courant[:, :, -8:], "lat", 1)

    slots = route(parcel_mass, parcel_owner, parcel_cell, devices, lats * lons)
    slots = lax.all_to_all(slots, ("lat", "lev"), split_axis=0, concat_axis=0, tiled=True)
    cap_lanes = slots.shape[2] - LANES
    blocks = cap_lanes // LANES
    rim_slots = shifted(slots, "lev", 1)

    def tables(slots, row):
        codes = slots[:, :blocks, cap_lanes:].astype(jnp.int32).reshape(devices * cap_lanes)
        counts = slots[:, row, cap_lanes].astype(jnp.int32)
        return codes, counts

    codes, counts = tables(slots, blocks)
    f0 = deposit(field, slots, codes, counts, 0, "deposit")
    codes, counts = tables(rim_slots, blocks + 1)
    rim = deposit(raw_rim[None], rim_slots, codes, counts, lats * lons // LANES, "deposit_rim")[0]
    halo = shifted(jnp.concatenate([rim[None, :, -8:], f0[:, :, -8:]], axis=0), "lat", 1)

    pairs = settle.reshape(bins, n_lev, 2)
    first, second = pairs[:, :, 0], pairs[:, :, 1]
    table = jnp.stack([first, 1.0 / (1.0 + first), second, 1.0 / (1.0 + second)], axis=0)
    params = lax.dynamic_index_in_dim(table, here, axis=2, keepdims=False).reshape(4 * bins)
    lam = (table[0] * table[1] * table[2] * table[3]).T
    lam = lax.dynamic_slice_in_dim(lam, here // cube * cube, cube, axis=0)
    gain = coag_gain + jnp.swapaxes(coag_gain, 1, 2)
    gain = jnp.where(jnp.eye(bins, dtype=bool)[None], coag_gain, gain)

    adv, hl = advance(params, f0, rim, halo, courant, courant_halo, courant_next)

    groups = [list(range(c * cube, (c + 1) * cube)) for c in range(cubes)]
    swap = functools.partial(
        lax.all_to_all, axis_name="lev", split_axis=0, concat_axis=0, axis_index_groups=groups, tiled=True
    )
    hl = swap(hl)
    flat_lam = lam.reshape(cube * bins)
    end = pl.pallas_call(
        cube_end_kernel,
        out_shape=jax.ShapeDtypeStruct(hl.shape[1:], jnp.float32),
        in_specs=[SMEM, VMEM],
        out_specs=VMEM,
        compiler_params=BIG,
        name="cube_end",
    )(flat_lam, hl)
    reach = 1
    factor = jnp.prod(lam, axis=0)[:, None, None]
    while reach < cubes - 1:
        end = end + factor * shifted(end, "lev", reach * cube)
        factor = factor * shifted(factor, "lev", reach * cube)
        reach = 2 * reach
    carried = shifted(end, "lev", cube)
    h = pl.pallas_call(
        cube_scan_kernel,
        out_shape=jax.ShapeDtypeStruct(hl.shape, jnp.float32),
        in_specs=[SMEM, VMEM, VMEM],
        out_specs=VMEM,
        compiler_params=BIG,
        name="cube_scan",
    )(flat_lam, hl, carried)
    h = swap(h)
    return finish(params, coag_loss.reshape(-1), gain.reshape(-1), adv, h)


def solution(mesh):
    in_specs = (
        P("lev", None, "lat", None),
        P(None, "lev", "lat", None),
        P(None, ("lat", "lev")),
        P(("lat", "lev"), None),
        P(("lat", "lev")),
        P(),
        P(),
        P(),
    )
    out_specs = P("lev", None, "lat", None)
    return jax.shard_map(
        on_device, mesh=mesh, in_specs=in_specs, out_specs=out_specs, check_vma=False
    )
```

```python
import functools

import jax
import jax.numpy as jnp
from jax import lax
from jax.experimental import pallas as pl
from jax.experimental.pallas import tpu as pltpu
from jax.sharding import PartitionSpec as P

ADV_STEPS = 2
LANES = 128
ROUTE_BLOCK = 256
ACCS = 4
ROWS = 32
HALVES = 2
VMEM = pl.BlockSpec(memory_space=pltpu.VMEM)
SMEM = pl.BlockSpec(memory_space=pltpu.SMEM)
BIG = pltpu.CompilerParams(vmem_limit_bytes=56 * 1024 * 1024)


def cost(us):
    return pl.CostEstimate(flops=int(us * 1.1e9), bytes_accessed=int(us * 3.6e6), transcendentals=0)


def route_kernel(devices, cap_lanes, level_cells, owner_ref, cell_ref, mass_ref, out_ref, a_ref, c_ref, b_ref):
    parcels = owner_ref.shape[1]
    blocks = cap_lanes // LANES
    width = ROUTE_BLOCK
    dev_ids = lax.broadcasted_iota(jnp.int32, (devices, width), 0)
    before = (
        lax.broadcasted_iota(jnp.int32, (width, width), 0) < lax.broadcasted_iota(jnp.int32, (width, width), 1)
    ).astype(jnp.bfloat16)
    slot_ids = lax.broadcasted_iota(jnp.int32, (cap_lanes, width), 0)

    def masks(start):
        owner = owner_ref[:, pl.ds(start, width)]
        cell = cell_ref[:, pl.ds(start, width)]
        mine = owner == dev_ids
        low = cell >= level_cells
        return owner, cell, jnp.where(mine & low, 1.0, 0.0), jnp.where(mine & (~low), 1.0, 0.0)

    low_total = jnp.zeros((devices, 1), jnp.float32)
    for start in range(0, parcels, width):
        unused, unused, low, high = masks(start)
        low_total = low_total + jnp.sum(low, axis=1, keepdims=True)
    low_base = jnp.zeros((devices, 1), jnp.float32)
    high_base = low_total
    for start in range(0, parcels, width):
        owner, cell, low, high = masks(start)
        both = jnp.concatenate([low, high], axis=0)
        earlier = jnp.dot(both.astype(jnp.bfloat16), before, preferred_element_type=jnp.float32)
        rank = jnp.sum(both * (earlier + jnp.concatenate([low_base, high_base], axis=0)), axis=0, keepdims=True)
        low_base = low_base + jnp.sum(low, axis=1, keepdims=True)
        high_base = high_base + jnp.sum(high, axis=1, keepdims=True)
        b_ref[:, pl.ds(start, width)] = jnp.where(slot_ids == rank.astype(jnp.int32), 1.0, 0.0).astype(jnp.bfloat16)
        mass = mass_ref[:, pl.ds(start, width)]
        coarse = mass.astype(jnp.bfloat16).astype(jnp.float32)
        fine = mass - coarse
        owner_rows = jnp.broadcast_to(owner, (8, width))
        for device in range(0, devices, 2):
            for part, piece in enumerate((coarse, fine)):
                pair = jnp.concatenate(
                    [jnp.where(owner_rows == device + extra, piece, 0.0) for extra in range(2)], axis=0
                )
                a_ref[pl.ds(part * devices * 8 + device * 8, 16), pl.ds(start, width)] = pair.astype(jnp.bfloat16)
        mine = low + high
        for part, piece in enumerate((cell >> 16, (cell >> 8) & 255, cell & 255)):
            c_ref[pl.ds(part * devices, devices), pl.ds(start, width)] = (mine * piece.astype(jnp.float32)).astype(
                jnp.bfloat16
            )
    contract = (((1,), (1,)), ((), ()))
    sorted_mass = lax.dot_general(a_ref[...], b_ref[...], contract, preferred_element_type=jnp.float32)
    sorted_cell = lax.dot_general(c_ref[...], b_ref[...], contract, preferred_element_type=jnp.float32)
    code = (
        sorted_cell[:devices] * 65536.0 + sorted_cell[devices : 2 * devices] * 256.0 + sorted_cell[2 * devices :]
    )
    total = sorted_mass[: devices * 8] + sorted_mass[devices * 8 :]
    out_ref[:, :, pl.ds(0, cap_lanes)] = total.reshape(devices, 8, cap_lanes)
    rows = lax.broadcasted_iota(jnp.int32, (8, LANES), 0)
    for device in range(devices):
        tile = jnp.zeros((8, LANES), jnp.float32)
        for block in range(blocks):
            tile = jnp.where(rows == block, code[device : device + 1, block * LANES : (block + 1) * LANES], tile)
        tile = jnp.where(rows == blocks, high_base[device : device + 1], tile)
        tile = jnp.where(rows == blocks + 1, low_base[device : device + 1], tile)
        out_ref[device, :, pl.ds(cap_lanes, LANES)] = tile


def route(parcel_mass, parcel_owner, parcel_cell, devices, level_cells):
    parcels = parcel_owner.shape[0]
    capacity = 2 * parcels // devices
    cap_lanes = -(-capacity // LANES) * LANES
    return pl.pallas_call(
        functools.partial(route_kernel, devices, cap_lanes, level_cells),
        out_shape=jax.ShapeDtypeStruct((devices, 8, cap_lanes + LANES), jnp.float32),
        in_specs=[VMEM] * 3,
        out_specs=VMEM,
        scratch_shapes=[
            pltpu.VMEM((devices * 16, parcels), jnp.bfloat16),
            pltpu.VMEM((devices * 3, parcels), jnp.bfloat16),
            pltpu.VMEM((cap_lanes, parcels), jnp.bfloat16),
        ],
        compiler_params=BIG,
        cost_estimate=cost(4),
        name="route",
    )(parcel_owner.reshape(1, parcels), parcel_cell.reshape(1, parcels), parcel_mass)


def deposit_kernel(with_field, rows_ref, counts_ref, slots_ref, *refs):
    if with_field:
        field_ref, *refs = refs
    out_ref, list_ref, pick_ref, even_ref, odd_ref, *accs = refs
    sources, unused, width = slots_ref.shape
    cap_lanes = width - LANES
    blocks = cap_lanes // LANES
    unused, bins, lats, lons = out_ref.shape
    lon_blocks = lons // LANES
    rows = accs[0].shape[0] - 8
    step = pl.program_id(0)

    @pl.when(step == 0)
    def collect():
        def clear(index, carry):
            for acc in accs:
                acc[pl.ds(index * 8, 8)] = jnp.zeros((8, 8, LANES), jnp.float32)
            return carry

        lax.fori_loop(0, rows // 8, clear, 0)
        pick_ref[...] = jnp.where(
            lax.broadcasted_iota(jnp.int32, pick_ref.shape, 0) // 8 == lax.broadcasted_iota(jnp.int32, pick_ref.shape, 1),
            1.0,
            0.0,
        ).astype(jnp.bfloat16)
        lane_ids = lax.broadcasted_iota(jnp.int32, (LANES, LANES), 0)
        tile_row = lax.broadcasted_iota(jnp.int32, (8, LANES), 0)

        def note(source, active):
            for block in range(blocks):
                list_ref[active] = source * blocks + block
                active = active + jnp.where(counts_ref[source] > block * LANES, 1, 0)
            return active

        active = lax.fori_loop(0, sources, note, 0)
        for extra in range(3):
            list_ref[active + extra] = 0

        def spread(index, spread_ref):
            item = list_ref[index]
            source = item // blocks
            block = item % blocks
            live = jnp.where(index < active, 1.0, 0.0)
            mass = slots_ref[source, :, pl.ds(pl.multiple_of(block * LANES, LANES), LANES)] * live
            code = slots_ref[source, :, pl.ds(cap_lanes, LANES)]
            code = jnp.sum(jnp.where(tile_row == block, code, 0.0), axis=0, keepdims=True).astype(jnp.int32)
            hot = jnp.where(lane_ids == (code & (LANES - 1)), 1.0, 0.0).astype(jnp.bfloat16)
            coarse = mass.astype(jnp.bfloat16).astype(jnp.float32)
            parts = [
                pick_ref[...] * jnp.tile(jnp.concatenate([part, part], axis=0).astype(jnp.bfloat16), (LANES // 2, 1))
                for part in (coarse, mass - coarse)
            ]
            spread_ref[...] = lax.dot_general(
                jnp.concatenate(parts, axis=1),
                jnp.concatenate([hot, hot], axis=1),
                (((1,), (1,)), ((), ())),
                preferred_element_type=jnp.float32,
            )

        def add(index, spread_ref):
            base = list_ref[index] * LANES
            for first in range(0, LANES, ACCS):
                places = [rows_ref[base + first + k] for k in range(ACCS)]
                held = [acc[place] for acc, place in zip(accs, places)]
                for k in range(ACCS):
                    accs[k][places[k]] = held[k] + spread_ref[(first + k) * 8 : (first + k + 1) * 8, :]

        spread(0, even_ref)

        def pair(index, carry):
            spread(2 * index + 1, odd_ref)
            add(2 * index, even_ref)
            spread(2 * index + 2, even_ref)
            add(2 * index + 1, odd_ref)
            return carry

        lax.fori_loop(0, (active + 1) // 2, pair, 0)

    @pl.when(step > 0)
    def merge():
        flat = [acc.reshape((rows + 8) * 8, LANES) for acc in accs]
        base = (step - 1) * lats * lon_blocks * 8
        for lat in range(0, lats, 8):
            for lon in range(lon_blocks):
                at = pl.ds(lon * LANES, LANES)
                for b in range(bins):
                    picked = pl.ds(base + (lat * lon_blocks + lon) * 8 + b, 8, stride=lon_blocks * 8)
                    total = flat[0][picked, :]
                    for acc in flat[1:]:
                        total = total + acc[picked, :]
                    if with_field:
                        total = total + field_ref[0, b, pl.ds(lat, 8), at]
                    out_ref[0, b, pl.ds(lat, 8), at] = total


def deposit(field, shape, slots, cell_rows, counts, name):
    levels, bins, lats, lons = shape
    rows = levels * lats * lons // LANES
    per = lats // ROWS

    def at(step):
        block = jnp.maximum(step - 1, 0)
        return (block // per, 0, block % per, 0)

    spec = pl.BlockSpec((1, bins, ROWS, lons), at)
    fields = [] if field is None else [field]
    return pl.pallas_call(
        functools.partial(deposit_kernel, bool(fields)),
        out_shape=jax.ShapeDtypeStruct(shape, jnp.float32),
        grid=(1 + levels * per,),
        in_specs=[SMEM, SMEM, VMEM] + [spec] * len(fields),
        out_specs=spec,
        scratch_shapes=[
            pltpu.SMEM((cell_rows.shape[0] // LANES + 8,), jnp.int32),
            pltpu.VMEM((8 * LANES, LANES), jnp.bfloat16),
            pltpu.VMEM((8 * LANES, LANES), jnp.float32),
            pltpu.VMEM((8 * LANES, LANES), jnp.float32),
        ]
        + [pltpu.VMEM((rows + 8, 8, LANES), jnp.float32)] * ACCS,
        compiler_params=BIG,
        cost_estimate=cost(22 if fields else 12),
        name=name,
    )(cell_rows, counts, slots, *fields)


def advance_kernel(
    first_bin, par_ref, f_ref, rim_ref, drop_ref, halo_ref, c_ref, ch_ref, cn_ref, adv_ref, hl_ref, p0, p1, keep_ref
):
    step = pl.program_id(0)
    unused, bins, lats, lons = f_ref.shape

    @pl.when(step == 0)
    def halo():
        def one(b, carry):
            above = halo_ref[0, b]
            for level in range(2):
                f = halo_ref[1 + level, b]
                rolled = pltpu.roll(f, 1, 0)
                p0[level, b] = rolled
                new = (
                    f
                    - ch_ref[0, level] * (f - pltpu.roll(f, 1, 1))
                    - ch_ref[1, level] * (f - rolled)
                    - ch_ref[2, level] * (f - above)
                )
                p1[level, b] = pltpu.roll(new, 1, 0)
                above = f
            return carry

        lax.fori_loop(0, bins, one, 0)

    @pl.when(step > 0)
    def main():
        top_row = lax.broadcasted_iota(jnp.int32, (8, lons), 0) == 0

        def south(prev, level, b, f):
            rolled = pltpu.roll(f, 1, 0)
            out = jnp.where(top_row, prev[level, b], rolled)
            prev[level, b] = rolled
            return out

        for lat in range(lats // 8):
            at = pl.ds(lat * 8, 8)

            keep = [1.0 - c_ref[0, level, at] - c_ref[1, level, at] - c_ref[2, level, at] for level in range(2)]
            for level in range(2):
                keep_ref[level] = keep[level]

            def flow(level, b, f, prev, above):
                new = (
                    keep_ref[level] * f
                    + c_ref[0, level, at] * pltpu.roll(f, 1, 1)
                    + c_ref[1, level, at] * south(prev, level, b, f)
                )
                return new if above is None else new + c_ref[2, level, at] * above

            def one(b, carry):
                scale = first_bin + b
                f0 = f_ref[0, b, at]
                f1 = f_ref[1, b, at]
                g0 = flow(0, b, f0, p0, rim_ref[b, at] + drop_ref[b, at])
                g1 = flow(1, b, f1, p0, f0)
                a0 = flow(0, b, g0, p1, None)
                a1 = flow(1, b, g1, p1, g0)
                adv_ref[0, b, at] = a0
                adv_ref[1, b, at] = a1
                low = (a1 + par_ref[scale] * (a0 * par_ref[8 + scale])) * par_ref[24 + scale]
                hl_ref[lat, b] = cn_ref[at] * g1 + par_ref[16 + scale] * low
                return carry

            lax.fori_loop(0, bins, one, 0)


def advance(half, params, field, rim, drop, halo, courant, courant_halo, courant_next):
    levels, all_bins, lats, lons = field.shape
    bins = all_bins // HALVES
    at = lambda step: jnp.maximum(step - 1, 0)
    return pl.pallas_call(
        functools.partial(advance_kernel, half * bins),
        out_shape=(
            jax.ShapeDtypeStruct((levels, bins, lats, lons), jnp.float32),
            jax.ShapeDtypeStruct((lats // 8, bins, 8, lons), jnp.float32),
        ),
        grid=(lats // ROWS + 1,),
        in_specs=[
            SMEM,
            pl.BlockSpec((levels, bins, ROWS, lons), lambda step: (0, half, at(step), 0)),
            pl.BlockSpec((bins, ROWS, lons), lambda step: (0, at(step), 0)),
            pl.BlockSpec((bins, ROWS, lons), lambda step: (half, at(step), 0)),
            pl.BlockSpec((3, bins, 8, lons), lambda step: (0, 0, 0, 0)),
            pl.BlockSpec((3, levels, ROWS, lons), lambda step: (0, 0, at(step), 0)),
            pl.BlockSpec((3, levels, 8, lons), lambda step: (0, 0, 0, 0)),
            pl.BlockSpec((ROWS, lons), lambda step: (at(step), 0)),
        ],
        out_specs=(
            pl.BlockSpec((levels, bins, ROWS, lons), lambda step: (0, 0, at(step), 0)),
            pl.BlockSpec((ROWS // 8, bins, 8, lons), lambda step: (at(step), 0, 0, 0)),
        ),
        scratch_shapes=[pltpu.VMEM((levels, bins, 8, lons), jnp.float32)] * 2 + [pltpu.VMEM((levels, 8, lons), jnp.float32)],
        compiler_params=BIG,
        cost_estimate=cost(9),
        name="advance",
    )(params, field, rim, drop, halo, courant, courant_halo, courant_next)


def cube_end_kernel(lam_ref, hl_ref, out_ref):
    count, bins = hl_ref.shape[:2]

    def one(b, carry):
        h = hl_ref[0, b]
        for member in range(1, count):
            h = hl_ref[member, b] + lam_ref[member * bins + b] * h
        out_ref[b] = h
        return carry

    lax.fori_loop(0, bins, one, 0)


def cube_scan_kernel(lam_ref, hl_ref, hin_ref, out_ref):
    count, bins = hl_ref.shape[:2]

    def one(b, carry):
        h = hin_ref[b]
        out_ref[0, b] = h
        for member in range(count - 1):
            h = hl_ref[member, b] + lam_ref[member * bins + b] * h
            out_ref[member + 1, b] = h
        return carry

    lax.fori_loop(0, bins, one, 0)


def finish_kernel(par_ref, loss_ref, gain_ref, *refs):
    *ins, out_ref = refs
    adv_refs, h_refs = ins[:HALVES], ins[HALVES:]
    unused, bins, lats, lons = out_ref.shape
    per = bins // HALVES
    width = 3 * LANES
    parts = lons // width

    def part(index, carry):
        lat = index // parts
        row = pl.ds(pl.multiple_of(lat * 8, 8), 8)
        at = pl.ds(pl.multiple_of((index % parts) * width, LANES), width)
        above = [h_refs[b // per][lat, b % per, :, at] for b in range(bins)]
        for level in range(2):
            solved = []
            for b in range(bins):
                s = (adv_refs[b // per][level, b % per, row, at] + above[b]) * par_ref[16 * level + 8 + b]
                solved.append(s)
                above[b] = par_ref[b] * s
            for i in range(bins):
                loss = loss_ref[i * bins] * solved[0]
                for j in range(1, bins):
                    loss = loss + loss_ref[i * bins + j] * solved[j]
                total = solved[i]
                base = i * bins * bins
                for j in range(bins):
                    inner = gain_ref[base + j * bins] * solved[0]
                    for k in range(1, j + 1):
                        inner = inner + gain_ref[base + j * bins + k] * solved[k]
                    total = total + inner * solved[j]
                out_ref[level, i, row, at] = total / (1.0 + loss)
        return carry

    lax.fori_loop(0, (lats // 8) * parts, part, 0)


def finish(params, loss, gain, adv, h):
    levels, per, lats, lons = adv[0].shape
    bins = per * HALVES
    rows = ROWS // 2
    return pl.pallas_call(
        finish_kernel,
        out_shape=jax.ShapeDtypeStruct((levels, bins, lats, lons), jnp.float32),
        grid=(lats // rows,),
        in_specs=[SMEM] * 3
        + [pl.BlockSpec((levels, per, rows, lons), lambda step: (0, 0, step, 0))] * HALVES
        + [pl.BlockSpec((rows // 8, per, 8, lons), lambda step: (step, 0, 0, 0))] * HALVES,
        out_specs=pl.BlockSpec((levels, bins, rows, lons), lambda step: (0, 0, step, 0)),
        compiler_params=BIG,
        cost_estimate=cost(18),
        name="finish",
    )(params, loss, gain, *adv, *h)


def shifted(value, axis, steps):
    count = lax.axis_size(axis)
    first, last = (max(0, -steps), min(count, count - steps))
    return lax.ppermute(value, axis, [(source, source + steps) for source in range(first, last)])


def on_device(field, courant, parcel_mass, parcel_owner, parcel_cell, settle, coag_gain, coag_loss):
    levels, bins, lats, lons = field.shape
    n_lev = lax.axis_size("lev")
    devices = lax.axis_size(("lat", "lev"))
    cube = lats // 8
    cubes = n_lev // cube
    here = lax.axis_index("lev")

    per = bins // HALVES
    early_rim = shifted(field[-1, :per], "lev", 1)
    courant_next = shifted(courant[2, 0], "lev", -1)
    courant_halo = shifted(courant[:, :, -8:], "lat", 1)

    slots = route(parcel_mass, parcel_owner, parcel_cell, devices, lats * lons)
    slots = lax.all_to_all(slots, ("lat", "lev"), split_axis=0, concat_axis=0, tiled=True)
    cap_lanes = slots.shape[2] - LANES
    blocks = cap_lanes // LANES
    level_rows = lats * lons // LANES
    rim_slots = shifted(slots, "lev", 1)

    def tables(slots, row):
        codes = slots[:, :blocks, cap_lanes:].astype(jnp.int32).reshape(devices * cap_lanes)
        counts = slots[:, row, cap_lanes].astype(jnp.int32)
        return codes // LANES, counts

    rows, counts = tables(slots, blocks)
    f0 = deposit(field, field.shape, slots, rows, counts, "deposit")
    rim_slots, later_rim = lax.optimization_barrier((rim_slots, field[-1, per:]))
    raw_rims = [early_rim, shifted(later_rim, "lev", 1)]
    rows, counts = tables(rim_slots, blocks + 1)
    rows = jnp.where(rows < level_rows, level_rows, rows - level_rows)
    drop = deposit(None, (1,) + field.shape[1:], rim_slots, rows, counts, "deposit_rim")[0]
    pairs = settle.reshape(bins, n_lev, 2)
    first, second = pairs[:, :, 0], pairs[:, :, 1]
    table = jnp.stack([first, 1.0 / (1.0 + first), second, 1.0 / (1.0 + second)], axis=0)
    params = lax.dynamic_index_in_dim(table, here, axis=2, keepdims=False).reshape(4 * bins)
    lam = (table[0] * table[1] * table[2] * table[3]).T
    lam = lax.dynamic_slice_in_dim(lam, here // cube * cube, cube, axis=0)
    gain = coag_gain + jnp.swapaxes(coag_gain, 1, 2)
    gain = jnp.where(jnp.eye(bins, dtype=bool)[None], coag_gain, gain)

    groups = [list(range(c * cube, (c + 1) * cube)) for c in range(cubes)]
    swap = functools.partial(
        lax.all_to_all, axis_name="lev", split_axis=0, concat_axis=0, axis_index_groups=groups, tiled=True
    )
    advs, hs = [], []
    for half in range(HALVES):
        own = slice(half * per, (half + 1) * per)
        raw_rim = raw_rims[half]
        if half:
            advs[-1], raw_rim = lax.optimization_barrier((advs[-1], raw_rim))
        rim_halo = raw_rim[:, -8:] + drop[own, -8:]
        halo = shifted(jnp.concatenate([rim_halo[None], f0[:, own, -8:]], axis=0), "lat", 1)
        adv, hl = advance(half, params, f0, raw_rim, drop, halo, courant, courant_halo, courant_next)
        advs.append(adv)
        hs.append(swap(hl))
    for half in range(HALVES):
        hs[half] = swap(carry_scan(hs[half], lam[:, half * per : (half + 1) * per], cubes))
    return finish(params, coag_loss.reshape(-1), gain.reshape(-1), advs, hs)


def carry_scan(hl, lam, cubes):
    cube = hl.shape[0]
    flat_lam = lam.reshape(-1)
    end = pl.pallas_call(
        cube_end_kernel,
        out_shape=jax.ShapeDtypeStruct(hl.shape[1:], jnp.float32),
        in_specs=[SMEM, VMEM],
        out_specs=VMEM,
        compiler_params=BIG,
        cost_estimate=cost(2),
        name="cube_end",
    )(flat_lam, hl)
    reach = 1
    factor = jnp.prod(lam, axis=0)[:, None, None]
    while reach < cubes - 1:
        end = end + factor * shifted(end, "lev", reach * cube)
        factor = factor * shifted(factor, "lev", reach * cube)
        reach = 2 * reach
    carried = shifted(end, "lev", cube)
    return pl.pallas_call(
        cube_scan_kernel,
        out_shape=jax.ShapeDtypeStruct(hl.shape, jnp.float32),
        in_specs=[SMEM, VMEM, VMEM],
        out_specs=VMEM,
        compiler_params=BIG,
        cost_estimate=cost(2),
        name="cube_scan",
    )(flat_lam, hl, carried)


def solution(mesh):
    in_specs = (
        P("lev", None, "lat", None),
        P(None, "lev", "lat", None),
        P(None, ("lat", "lev")),
        P(("lat", "lev"), None),
        P(("lat", "lev")),
        P(),
        P(),
        P(),
    )
    out_specs = P("lev", None, "lat", None)
    return jax.shard_map(
        on_device, mesh=mesh, in_specs=in_specs, out_specs=out_specs, check_vma=False
    )
```

```python
import functools

import jax
import jax.numpy as jnp
from jax import lax
from jax.experimental import pallas as pl
from jax.experimental.pallas import tpu as pltpu
from jax.sharding import PartitionSpec as P

ADV_STEPS = 2
LANES = 128
ROUTE_BLOCK = 256
ACCS = 4
ROWS = 32
HALVES = 2
VMEM = pl.BlockSpec(memory_space=pltpu.VMEM)
SMEM = pl.BlockSpec(memory_space=pltpu.SMEM)
BIG = pltpu.CompilerParams(vmem_limit_bytes=56 * 1024 * 1024)


def cost(us):
    return pl.CostEstimate(flops=int(us * 1.1e9), bytes_accessed=int(us * 3.6e6), transcendentals=0)


def route_kernel(devices, cap_lanes, level_cells, owner_ref, cell_ref, mass_ref, out_ref, a_ref, c_ref, b_ref):
    parcels = owner_ref.shape[1]
    blocks = cap_lanes // LANES
    width = ROUTE_BLOCK
    dev_ids = lax.broadcasted_iota(jnp.int32, (devices, width), 0)
    before = (
        lax.broadcasted_iota(jnp.int32, (width, width), 0) < lax.broadcasted_iota(jnp.int32, (width, width), 1)
    ).astype(jnp.bfloat16)
    slot_ids = lax.broadcasted_iota(jnp.int32, (cap_lanes, width), 0)

    def masks(start):
        owner = owner_ref[:, pl.ds(start, width)]
        cell = cell_ref[:, pl.ds(start, width)]
        mine = owner == dev_ids
        low = cell >= level_cells
        return owner, cell, jnp.where(mine & low, 1.0, 0.0), jnp.where(mine & (~low), 1.0, 0.0)

    low_total = jnp.zeros((devices, 1), jnp.float32)
    for start in range(0, parcels, width):
        unused, unused, low, high = masks(start)
        low_total = low_total + jnp.sum(low, axis=1, keepdims=True)
    low_base = jnp.zeros((devices, 1), jnp.float32)
    high_base = low_total
    for start in range(0, parcels, width):
        owner, cell, low, high = masks(start)
        both = jnp.concatenate([low, high], axis=0)
        earlier = jnp.dot(both.astype(jnp.bfloat16), before, preferred_element_type=jnp.float32)
        rank = jnp.sum(both * (earlier + jnp.concatenate([low_base, high_base], axis=0)), axis=0, keepdims=True)
        low_base = low_base + jnp.sum(low, axis=1, keepdims=True)
        high_base = high_base + jnp.sum(high, axis=1, keepdims=True)
        b_ref[:, pl.ds(start, width)] = jnp.where(slot_ids == rank.astype(jnp.int32), 1.0, 0.0).astype(jnp.bfloat16)
        mass = mass_ref[:, pl.ds(start, width)]
        coarse = mass.astype(jnp.bfloat16).astype(jnp.float32)
        fine = mass - coarse
        owner_rows = jnp.broadcast_to(owner, (8, width))
        for device in range(0, devices, 2):
            for part, piece in enumerate((coarse, fine)):
                pair = jnp.concatenate(
                    [jnp.where(owner_rows == device + extra, piece, 0.0) for extra in range(2)], axis=0
                )
                a_ref[pl.ds(part * devices * 8 + device * 8, 16), pl.ds(start, width)] = pair.astype(jnp.bfloat16)
        mine = low + high
        for part, piece in enumerate((cell >> 16, (cell >> 8) & 255, cell & 255)):
            c_ref[pl.ds(part * devices, devices), pl.ds(start, width)] = (mine * piece.astype(jnp.float32)).astype(
                jnp.bfloat16
            )
    contract = (((1,), (1,)), ((), ()))
    sorted_mass = lax.dot_general(a_ref[...], b_ref[...], contract, preferred_element_type=jnp.float32)
    sorted_cell = lax.dot_general(c_ref[...], b_ref[...], contract, preferred_element_type=jnp.float32)
    code = (
        sorted_cell[:devices] * 65536.0 + sorted_cell[devices : 2 * devices] * 256.0 + sorted_cell[2 * devices :]
    )
    total = sorted_mass[: devices * 8] + sorted_mass[devices * 8 :]
    out_ref[:, :, pl.ds(0, cap_lanes)] = total.reshape(devices, 8, cap_lanes)
    rows = lax.broadcasted_iota(jnp.int32, (8, LANES), 0)
    for device in range(devices):
        tile = jnp.zeros((8, LANES), jnp.float32)
        for block in range(blocks):
            tile = jnp.where(rows == block, code[device : device + 1, block * LANES : (block + 1) * LANES], tile)
        tile = jnp.where(rows == blocks, high_base[device : device + 1], tile)
        tile = jnp.where(rows == blocks + 1, low_base[device : device + 1], tile)
        out_ref[device, :, pl.ds(cap_lanes, LANES)] = tile


def route(parcel_mass, parcel_owner, parcel_cell, devices, level_cells):
    parcels = parcel_owner.shape[0]
    capacity = 2 * parcels // devices
    cap_lanes = -(-capacity // LANES) * LANES
    return pl.pallas_call(
        functools.partial(route_kernel, devices, cap_lanes, level_cells),
        out_shape=jax.ShapeDtypeStruct((devices, 8, cap_lanes + LANES), jnp.float32),
        in_specs=[VMEM] * 3,
        out_specs=VMEM,
        scratch_shapes=[
            pltpu.VMEM((devices * 16, parcels), jnp.bfloat16),
            pltpu.VMEM((devices * 3, parcels), jnp.bfloat16),
            pltpu.VMEM((cap_lanes, parcels), jnp.bfloat16),
        ],
        compiler_params=BIG,
        cost_estimate=cost(4),
        name="route",
    )(parcel_owner.reshape(1, parcels), parcel_cell.reshape(1, parcels), parcel_mass)


def deposit_kernel(with_field, rows_ref, counts_ref, slots_ref, *refs):
    if with_field:
        field_ref, *refs = refs
    out_ref, list_ref, pick_ref, even_ref, odd_ref, *accs = refs
    sources, unused, width = slots_ref.shape
    cap_lanes = width - LANES
    blocks = cap_lanes // LANES
    unused, bins, lats, lons = out_ref.shape
    lon_blocks = lons // LANES
    rows = accs[0].shape[0] - 8
    step = pl.program_id(0)

    @pl.when(step == 0)
    def collect():
        def clear(index, carry):
            for acc in accs:
                acc[pl.ds(index * 8, 8)] = jnp.zeros((8, 8, LANES), jnp.float32)
            return carry

        lax.fori_loop(0, rows // 8, clear, 0)
        pick_ref[...] = jnp.where(
            lax.broadcasted_iota(jnp.int32, pick_ref.shape, 0) // 8 == lax.broadcasted_iota(jnp.int32, pick_ref.shape, 1),
            1.0,
            0.0,
        ).astype(jnp.bfloat16)
        lane_ids = lax.broadcasted_iota(jnp.int32, (LANES, LANES), 0)
        tile_row = lax.broadcasted_iota(jnp.int32, (8, LANES), 0)

        def note(source, active):
            for block in range(blocks):
                list_ref[active] = source * blocks + block
                active = active + jnp.where(counts_ref[source] > block * LANES, 1, 0)
            return active

        active = lax.fori_loop(0, sources, note, 0)
        for extra in range(3):
            list_ref[active + extra] = 0

        def spread(index, spread_ref):
            item = list_ref[index]
            source = item // blocks
            block = item % blocks
            live = jnp.where(index < active, 1.0, 0.0)
            mass = slots_ref[source, :, pl.ds(pl.multiple_of(block * LANES, LANES), LANES)] * live
            code = slots_ref[source, :, pl.ds(cap_lanes, LANES)]
            code = jnp.sum(jnp.where(tile_row == block, code, 0.0), axis=0, keepdims=True).astype(jnp.int32)
            hot = jnp.where(lane_ids == (code & (LANES - 1)), 1.0, 0.0).astype(jnp.bfloat16)
            coarse = mass.astype(jnp.bfloat16).astype(jnp.float32)
            parts = [
                pick_ref[...] * jnp.tile(jnp.concatenate([part, part], axis=0).astype(jnp.bfloat16), (LANES // 2, 1))
                for part in (coarse, mass - coarse)
            ]
            spread_ref[...] = lax.dot_general(
                jnp.concatenate(parts, axis=1),
                jnp.concatenate([hot, hot], axis=1),
                (((1,), (1,)), ((), ())),
                preferred_element_type=jnp.float32,
            )

        def add(index, spread_ref):
            base = list_ref[index] * LANES
            for first in range(0, LANES, ACCS):
                places = [rows_ref[base + first + k] for k in range(ACCS)]
                held = [acc[place] for acc, place in zip(accs, places)]
                for k in range(ACCS):
                    accs[k][places[k]] = held[k] + spread_ref[(first + k) * 8 : (first + k + 1) * 8, :]

        spread(0, even_ref)

        def pair(index, carry):
            spread(2 * index + 1, odd_ref)
            add(2 * index, even_ref)
            spread(2 * index + 2, even_ref)
            add(2 * index + 1, odd_ref)
            return carry

        lax.fori_loop(0, (active + 1) // 2, pair, 0)

    @pl.when(step > 0)
    def merge():
        flat = [acc.reshape((rows + 8) * 8, LANES) for acc in accs]
        base = (step - 1) * lats * lon_blocks * 8
        for lat in range(0, lats, 8):
            for lon in range(lon_blocks):
                at = pl.ds(lon * LANES, LANES)
                for b in range(bins):
                    picked = pl.ds(base + (lat * lon_blocks + lon) * 8 + b, 8, stride=lon_blocks * 8)
                    total = flat[0][picked, :]
                    for acc in flat[1:]:
                        total = total + acc[picked, :]
                    if with_field:
                        total = total + field_ref[0, b, pl.ds(lat, 8), at]
                    out_ref[0, b, pl.ds(lat, 8), at] = total


def deposit(field, shape, slots, cell_rows, counts, name):
    levels, bins, lats, lons = shape
    rows = levels * lats * lons // LANES
    per = lats // ROWS

    def at(step):
        block = jnp.maximum(step - 1, 0)
        return (block // per, 0, block % per, 0)

    spec = pl.BlockSpec((1, bins, ROWS, lons), at)
    fields = [] if field is None else [field]
    return pl.pallas_call(
        functools.partial(deposit_kernel, bool(fields)),
        out_shape=jax.ShapeDtypeStruct(shape, jnp.float32),
        grid=(1 + levels * per,),
        in_specs=[SMEM, SMEM, VMEM] + [spec] * len(fields),
        out_specs=spec,
        scratch_shapes=[
            pltpu.SMEM((cell_rows.shape[0] // LANES + 8,), jnp.int32),
            pltpu.VMEM((8 * LANES, LANES), jnp.bfloat16),
            pltpu.VMEM((8 * LANES, LANES), jnp.float32),
            pltpu.VMEM((8 * LANES, LANES), jnp.float32),
        ]
        + [pltpu.VMEM((rows + 8, 8, LANES), jnp.float32)] * ACCS,
        compiler_params=BIG,
        cost_estimate=cost(22 if fields else 12),
        name=name,
    )(cell_rows, counts, slots, *fields)


def advance_kernel(
    first_bin, par_ref, f_ref, rim_ref, drop_ref, halo_ref, c_ref, ch_ref, cn_ref, adv_ref, hl_ref, p0, p1, keep_ref
):
    step = pl.program_id(0)
    unused, bins, lats, lons = f_ref.shape

    @pl.when(step == 0)
    def halo():
        def one(b, carry):
            above = halo_ref[0, b]
            for level in range(2):
                f = halo_ref[1 + level, b]
                rolled = pltpu.roll(f, 1, 0)
                p0[level, b] = rolled
                new = (
                    f
                    - ch_ref[0, level] * (f - pltpu.roll(f, 1, 1))
                    - ch_ref[1, level] * (f - rolled)
                    - ch_ref[2, level] * (f - above)
                )
                p1[level, b] = pltpu.roll(new, 1, 0)
                above = f
            return carry

        lax.fori_loop(0, bins, one, 0)

    @pl.when(step > 0)
    def main():
        top_row = lax.broadcasted_iota(jnp.int32, (8, lons), 0) == 0

        def south(prev, level, b, f):
            rolled = pltpu.roll(f, 1, 0)
            out = jnp.where(top_row, prev[level, b], rolled)
            prev[level, b] = rolled
            return out

        for lat in range(lats // 8):
            at = pl.ds(lat * 8, 8)

            keep = [1.0 - c_ref[0, level, at] - c_ref[1, level, at] - c_ref[2, level, at] for level in range(2)]
            for level in range(2):
                keep_ref[level] = keep[level]

            def flow(level, b, f, prev, above):
                new = (
                    keep_ref[level] * f
                    + c_ref[0, level, at] * pltpu.roll(f, 1, 1)
                    + c_ref[1, level, at] * south(prev, level, b, f)
                )
                return new if above is None else new + c_ref[2, level, at] * above

            def one(b, carry):
                scale = first_bin + b
                f0 = f_ref[0, b, at]
                f1 = f_ref[1, b, at]
                g0 = flow(0, b, f0, p0, rim_ref[b, at] + drop_ref[b, at])
                g1 = flow(1, b, f1, p0, f0)
                a0 = flow(0, b, g0, p1, None)
                a1 = flow(1, b, g1, p1, g0)
                adv_ref[0, b, at] = a0
                adv_ref[1, b, at] = a1
                low = (a1 + par_ref[scale] * (a0 * par_ref[8 + scale])) * par_ref[24 + scale]
                hl_ref[lat, b] = cn_ref[at] * g1 + par_ref[16 + scale] * low
                return carry

            lax.fori_loop(0, bins, one, 0)


def advance(half, params, field, rim, drop, halo, courant, courant_halo, courant_next):
    levels, all_bins, lats, lons = field.shape
    bins = all_bins // HALVES
    at = lambda step: jnp.maximum(step - 1, 0)
    return pl.pallas_call(
        functools.partial(advance_kernel, half * bins),
        out_shape=(
            jax.ShapeDtypeStruct((levels, bins, lats, lons), jnp.float32),
            jax.ShapeDtypeStruct((lats // 8, bins, 8, lons), jnp.float32),
        ),
        grid=(lats // ROWS + 1,),
        in_specs=[
            SMEM,
            pl.BlockSpec((levels, bins, ROWS, lons), lambda step: (0, half, at(step), 0)),
            pl.BlockSpec((bins, ROWS, lons), lambda step: (0, at(step), 0)),
            pl.BlockSpec((bins, ROWS, lons), lambda step: (half, at(step), 0)),
            pl.BlockSpec((3, bins, 8, lons), lambda step: (0, 0, 0, 0)),
            pl.BlockSpec((3, levels, ROWS, lons), lambda step: (0, 0, at(step), 0)),
            pl.BlockSpec((3, levels, 8, lons), lambda step: (0, 0, 0, 0)),
            pl.BlockSpec((ROWS, lons), lambda step: (at(step), 0)),
        ],
        out_specs=(
            pl.BlockSpec((levels, bins, ROWS, lons), lambda step: (0, 0, at(step), 0)),
            pl.BlockSpec((ROWS // 8, bins, 8, lons), lambda step: (at(step), 0, 0, 0)),
        ),
        scratch_shapes=[pltpu.VMEM((levels, bins, 8, lons), jnp.float32)] * 2 + [pltpu.VMEM((levels, 8, lons), jnp.float32)],
        compiler_params=BIG,
        cost_estimate=cost(9),
        name="advance",
    )(params, field, rim, drop, halo, courant, courant_halo, courant_next)


def cube_end_kernel(lam_ref, hl_ref, out_ref):
    count, bins = hl_ref.shape[:2]

    def one(b, carry):
        h = hl_ref[0, b]
        for member in range(1, count):
            h = hl_ref[member, b] + lam_ref[member * bins + b] * h
        out_ref[b] = h
        return carry

    lax.fori_loop(0, bins, one, 0)


def cube_scan_kernel(lam_ref, hl_ref, hin_ref, out_ref):
    count, bins = hl_ref.shape[:2]

    def one(b, carry):
        h = hin_ref[b]
        out_ref[0, b] = h
        for member in range(count - 1):
            h = hl_ref[member, b] + lam_ref[member * bins + b] * h
            out_ref[member + 1, b] = h
        return carry

    lax.fori_loop(0, bins, one, 0)


def finish_kernel(par_ref, mix_ref, *refs):
    *ins, out_ref = refs
    adv_refs, h_refs = ins[:HALVES], ins[HALVES:]
    unused, bins, lats, lons = out_ref.shape
    per = bins // HALVES
    tiles = range(lats // 8)

    def part(index, carry):
        at = pl.ds(pl.multiple_of(index * LANES, LANES), LANES)
        above = [jnp.concatenate([h_refs[b // per][t, b % per, :, at] for t in tiles], axis=1) for b in range(bins)]
        for level in range(2):
            solved = []
            for b in range(bins):
                adv = [adv_refs[b // per][level, b % per, t * 8 : t * 8 + 8, at] for t in tiles]
                s = (jnp.concatenate(adv, axis=1) + above[b]) * par_ref[16 * level + 8 + b]
                solved.append(s)
                above[b] = par_ref[b] * s
            whole = jnp.concatenate(solved, axis=0)
            coarse = whole.astype(jnp.bfloat16)
            fine = (whole - coarse.astype(jnp.float32)).astype(jnp.bfloat16)
            mixed = jnp.dot(
                mix_ref[...], jnp.concatenate([coarse, coarse, fine], axis=0), preferred_element_type=jnp.float32
            )
            for i in range(bins):
                total = solved[i]
                for j in range(bins):
                    row = 8 * (bins + i * bins + j)
                    total = total + mixed[row : row + 8] * solved[j]
                total = total / (1.0 + mixed[8 * i : 8 * i + 8])
                for t in tiles:
                    out_ref[level, i, t * 8 : t * 8 + 8, at] = total[:, t * LANES : (t + 1) * LANES]
        return carry

    lax.fori_loop(0, lons // LANES, part, 0, unroll=True)


def mixing(coag_loss, coag_gain):
    bins = coag_loss.shape[0]
    both = jnp.concatenate([coag_loss, coag_gain.reshape(bins * bins, bins)], axis=0)
    eye = jnp.eye(8, dtype=jnp.float32)
    matrix = (both[:, None, :, None] * eye[None, :, None, :]).reshape(both.shape[0] * 8, bins * 8)
    coarse = matrix.astype(jnp.bfloat16)
    fine = (matrix - coarse.astype(jnp.float32)).astype(jnp.bfloat16)
    return jnp.concatenate([coarse, fine, coarse], axis=1)


def finish(params, mix, adv, h):
    levels, per, lats, lons = adv[0].shape
    bins = per * HALVES
    rows = ROWS // 2
    return pl.pallas_call(
        finish_kernel,
        out_shape=jax.ShapeDtypeStruct((levels, bins, lats, lons), jnp.float32),
        grid=(lats // rows,),
        in_specs=[SMEM, VMEM]
        + [pl.BlockSpec((levels, per, rows, lons), lambda step: (0, 0, step, 0))] * HALVES
        + [pl.BlockSpec((rows // 8, per, 8, lons), lambda step: (step, 0, 0, 0))] * HALVES,
        out_specs=pl.BlockSpec((levels, bins, rows, lons), lambda step: (0, 0, step, 0)),
        compiler_params=BIG,
        cost_estimate=cost(10),
        name="finish",
    )(params, mix, *adv, *h)


def shifted(value, axis, steps):
    count = lax.axis_size(axis)
    first, last = (max(0, -steps), min(count, count - steps))
    return lax.ppermute(value, axis, [(source, source + steps) for source in range(first, last)])


def on_device(field, courant, parcel_mass, parcel_owner, parcel_cell, settle, coag_gain, coag_loss):
    levels, bins, lats, lons = field.shape
    n_lev = lax.axis_size("lev")
    devices = lax.axis_size(("lat", "lev"))
    cube = lats // 8
    cubes = n_lev // cube
    here = lax.axis_index("lev")

    per = bins // HALVES
    early_rim = shifted(field[-1, :per], "lev", 1)
    slots = route(parcel_mass, parcel_owner, parcel_cell, devices, lats * lons)
    slots, courant = lax.optimization_barrier((slots, courant))
    courant_next = shifted(courant[2, 0], "lev", -1)
    courant_halo = shifted(courant[:, :, -8:], "lat", 1)
    slots = lax.all_to_all(slots, ("lat", "lev"), split_axis=0, concat_axis=0, tiled=True)
    cap_lanes = slots.shape[2] - LANES
    blocks = cap_lanes // LANES
    level_rows = lats * lons // LANES
    rim_slots = shifted(slots, "lev", 1)

    def tables(slots, row):
        codes = slots[:, :blocks, cap_lanes:].astype(jnp.int32).reshape(devices * cap_lanes)
        counts = slots[:, row, cap_lanes].astype(jnp.int32)
        return codes // LANES, counts

    rows, counts = tables(slots, blocks)
    f0 = deposit(field, field.shape, slots, rows, counts, "deposit")
    rim_slots, later_rim = lax.optimization_barrier((rim_slots, field[-1, per:]))
    raw_rims = [early_rim, shifted(later_rim, "lev", 1)]
    rows, counts = tables(rim_slots, blocks + 1)
    rows = jnp.where(rows < level_rows, level_rows, rows - level_rows)
    drop = deposit(None, (1,) + field.shape[1:], rim_slots, rows, counts, "deposit_rim")[0]
    pairs = settle.reshape(bins, n_lev, 2)
    first, second = pairs[:, :, 0], pairs[:, :, 1]
    table = jnp.stack([first, 1.0 / (1.0 + first), second, 1.0 / (1.0 + second)], axis=0)
    params = lax.dynamic_index_in_dim(table, here, axis=2, keepdims=False).reshape(4 * bins)
    lam = (table[0] * table[1] * table[2] * table[3]).T
    lam = lax.dynamic_slice_in_dim(lam, here // cube * cube, cube, axis=0)
    mix = mixing(coag_loss, coag_gain)

    groups = [list(range(c * cube, (c + 1) * cube)) for c in range(cubes)]
    swap = functools.partial(
        lax.all_to_all, axis_name="lev", split_axis=0, concat_axis=0, axis_index_groups=groups, tiled=True
    )
    advs, hs = [], []
    for half in range(HALVES):
        own = slice(half * per, (half + 1) * per)
        raw_rim = raw_rims[half]
        if half:
            advs[-1], raw_rim = lax.optimization_barrier((advs[-1], raw_rim))
        rim_halo = raw_rim[:, -8:] + drop[own, -8:]
        halo = shifted(jnp.concatenate([rim_halo[None], f0[:, own, -8:]], axis=0), "lat", 1)
        adv, hl = advance(half, params, f0, raw_rim, drop, halo, courant, courant_halo, courant_next)
        advs.append(adv)
        hs.append(swap(hl))
    for half in range(HALVES):
        hs[half] = swap(carry_scan(hs[half], lam[:, half * per : (half + 1) * per], cubes))
    return finish(params, mix, advs, hs)


def carry_scan(hl, lam, cubes):
    cube = hl.shape[0]
    flat_lam = lam.reshape(-1)
    end = pl.pallas_call(
        cube_end_kernel,
        out_shape=jax.ShapeDtypeStruct(hl.shape[1:], jnp.float32),
        in_specs=[SMEM, VMEM],
        out_specs=VMEM,
        compiler_params=BIG,
        cost_estimate=cost(2),
        name="cube_end",
    )(flat_lam, hl)
    reach = 1
    factor = jnp.prod(lam, axis=0)[:, None, None]
    while reach < cubes - 1:
        end = end + factor * shifted(end, "lev", reach * cube)
        factor = factor * shifted(factor, "lev", reach * cube)
        reach = 2 * reach
    carried = shifted(end, "lev", cube)
    return pl.pallas_call(
        cube_scan_kernel,
        out_shape=jax.ShapeDtypeStruct(hl.shape, jnp.float32),
        in_specs=[SMEM, VMEM, VMEM],
        out_specs=VMEM,
        compiler_params=BIG,
        cost_estimate=cost(2),
        name="cube_scan",
    )(flat_lam, hl, carried)


def solution(mesh):
    in_specs = (
        P("lev", None, "lat", None),
        P(None, "lev", "lat", None),
        P(None, ("lat", "lev")),
        P(("lat", "lev"), None),
        P(("lat", "lev")),
        P(),
        P(),
        P(),
    )
    out_specs = P("lev", None, "lat", None)
    return jax.shard_map(
        on_device, mesh=mesh, in_specs=in_specs, out_specs=out_specs, check_vma=False
    )
```

```python
import functools

import jax
import jax.numpy as jnp
from jax import lax
from jax.experimental import pallas as pl
from jax.experimental.pallas import tpu as pltpu
from jax.sharding import PartitionSpec as P

ADV_STEPS = 2
LANES = 128
ROUTE_BLOCK = 256
ACCS = 4
ROWS = 32
MERGE_ROWS = 64
HALVES = 2
VMEM = pl.BlockSpec(memory_space=pltpu.VMEM)
SMEM = pl.BlockSpec(memory_space=pltpu.SMEM)
BIG = pltpu.CompilerParams(vmem_limit_bytes=56 * 1024 * 1024)


def cost(us):
    return pl.CostEstimate(flops=int(us * 1.1e9), bytes_accessed=int(us * 3.6e6), transcendentals=0)


def route_kernel(devices, cap_lanes, level_cells, owner_ref, cell_ref, mass_ref, out_ref, a_ref, c_ref, b_ref):
    parcels = owner_ref.shape[1]
    blocks = cap_lanes // LANES
    width = ROUTE_BLOCK
    dev_ids = lax.broadcasted_iota(jnp.int32, (devices, width), 0)
    before = (
        lax.broadcasted_iota(jnp.int32, (width, width), 0) < lax.broadcasted_iota(jnp.int32, (width, width), 1)
    ).astype(jnp.bfloat16)
    slot_ids = lax.broadcasted_iota(jnp.int32, (cap_lanes, width), 0)

    def masks(start):
        owner = owner_ref[:, pl.ds(start, width)]
        cell = cell_ref[:, pl.ds(start, width)]
        mine = owner == dev_ids
        low = cell >= level_cells
        return owner, cell, jnp.where(mine & low, 1.0, 0.0), jnp.where(mine & (~low), 1.0, 0.0)

    low_total = jnp.zeros((devices, 1), jnp.float32)
    for start in range(0, parcels, width):
        unused, unused, low, high = masks(start)
        low_total = low_total + jnp.sum(low, axis=1, keepdims=True)
    low_base = jnp.zeros((devices, 1), jnp.float32)
    high_base = low_total
    for start in range(0, parcels, width):
        owner, cell, low, high = masks(start)
        both = jnp.concatenate([low, high], axis=0)
        earlier = jnp.dot(both.astype(jnp.bfloat16), before, preferred_element_type=jnp.float32)
        rank = jnp.sum(both * (earlier + jnp.concatenate([low_base, high_base], axis=0)), axis=0, keepdims=True)
        low_base = low_base + jnp.sum(low, axis=1, keepdims=True)
        high_base = high_base + jnp.sum(high, axis=1, keepdims=True)
        b_ref[:, pl.ds(start, width)] = jnp.where(slot_ids == rank.astype(jnp.int32), 1.0, 0.0).astype(jnp.bfloat16)
        mass = mass_ref[:, pl.ds(start, width)]
        coarse = mass.astype(jnp.bfloat16).astype(jnp.float32)
        fine = mass - coarse
        owner_rows = jnp.broadcast_to(owner, (8, width))
        for device in range(0, devices, 2):
            for part, piece in enumerate((coarse, fine)):
                pair = jnp.concatenate(
                    [jnp.where(owner_rows == device + extra, piece, 0.0) for extra in range(2)], axis=0
                )
                a_ref[pl.ds(part * devices * 8 + device * 8, 16), pl.ds(start, width)] = pair.astype(jnp.bfloat16)
        mine = low + high
        for part, piece in enumerate((cell >> 16, (cell >> 8) & 255, cell & 255)):
            c_ref[pl.ds(part * devices, devices), pl.ds(start, width)] = (mine * piece.astype(jnp.float32)).astype(
                jnp.bfloat16
            )
    contract = (((1,), (1,)), ((), ()))
    sorted_mass = lax.dot_general(a_ref[...], b_ref[...], contract, preferred_element_type=jnp.float32)
    sorted_cell = lax.dot_general(c_ref[...], b_ref[...], contract, preferred_element_type=jnp.float32)
    code = (
        sorted_cell[:devices] * 65536.0 + sorted_cell[devices : 2 * devices] * 256.0 + sorted_cell[2 * devices :]
    )
    total = sorted_mass[: devices * 8] + sorted_mass[devices * 8 :]
    out_ref[:, :, pl.ds(0, cap_lanes)] = total.reshape(devices, 8, cap_lanes)
    rows = lax.broadcasted_iota(jnp.int32, (8, LANES), 0)
    for device in range(devices):
        tile = jnp.zeros((8, LANES), jnp.float32)
        for block in range(blocks):
            tile = jnp.where(rows == block, code[device : device + 1, block * LANES : (block + 1) * LANES], tile)
        tile = jnp.where(rows == blocks, high_base[device : device + 1], tile)
        tile = jnp.where(rows == blocks + 1, low_base[device : device + 1], tile)
        out_ref[device, :, pl.ds(cap_lanes, LANES)] = tile


def route(parcel_mass, parcel_owner, parcel_cell, devices, level_cells):
    parcels = parcel_owner.shape[0]
    capacity = 2 * parcels // devices
    cap_lanes = -(-capacity // LANES) * LANES
    return pl.pallas_call(
        functools.partial(route_kernel, devices, cap_lanes, level_cells),
        out_shape=jax.ShapeDtypeStruct((devices, 8, cap_lanes + LANES), jnp.float32),
        in_specs=[VMEM] * 3,
        out_specs=VMEM,
        scratch_shapes=[
            pltpu.VMEM((devices * 16, parcels), jnp.bfloat16),
            pltpu.VMEM((devices * 3, parcels), jnp.bfloat16),
            pltpu.VMEM((cap_lanes, parcels), jnp.bfloat16),
        ],
        compiler_params=BIG,
        cost_estimate=cost(4),
        name="route",
    )(parcel_owner.reshape(1, parcels), parcel_cell.reshape(1, parcels), parcel_mass)


def deposit_kernel(with_field, item, rows_ref, counts_ref, slots_ref, *refs):
    if with_field:
        field_ref, *refs = refs
    out_ref, list_ref, pick_ref, even_ref, odd_ref, *accs = refs
    sources, unused, width = slots_ref.shape
    cap_lanes = width - LANES
    pieces = cap_lanes // item
    unused, bins, lats, lons = out_ref.shape
    lon_blocks = lons // LANES
    rows = accs[0].shape[0] - 8
    step = pl.program_id(0)

    @pl.when(step == 0)
    def collect():
        def clear(index, carry):
            for acc in accs:
                acc[pl.ds(index * 8, 8)] = jnp.zeros((8, 8, LANES), jnp.float32)
            return carry

        lax.fori_loop(0, rows // 8, clear, 0)
        pick_ref[...] = jnp.where(
            lax.broadcasted_iota(jnp.int32, pick_ref.shape, 0) // 8 == lax.broadcasted_iota(jnp.int32, pick_ref.shape, 1),
            1.0,
            0.0,
        ).astype(jnp.bfloat16)
        lane_ids = lax.broadcasted_iota(jnp.int32, (LANES, LANES), 0)
        tile_row = lax.broadcasted_iota(jnp.int32, (8, LANES), 0)

        def note(source, active):
            for piece in range(pieces):
                list_ref[active] = source * pieces + piece
                active = active + jnp.where(counts_ref[source] > piece * item, 1, 0)
            return active

        active = lax.fori_loop(0, sources, note, 0)
        for extra in range(3):
            list_ref[active + extra] = 0

        def spread(index, spread_ref):
            entry = list_ref[index]
            source = entry // pieces
            piece = entry % pieces
            block = piece * item // LANES
            picked = pl.ds(pl.multiple_of(piece % (LANES // item) * (8 * item), 8 * item), 8 * item)
            live = jnp.where(index < active, 1.0, 0.0)
            mass = slots_ref[source, :, pl.ds(pl.multiple_of(block * LANES, LANES), LANES)] * live
            code = slots_ref[source, :, pl.ds(cap_lanes, LANES)]
            code = jnp.sum(jnp.where(tile_row == block, code, 0.0), axis=0, keepdims=True).astype(jnp.int32)
            hot = jnp.where(lane_ids == (code & (LANES - 1)), 1.0, 0.0).astype(jnp.bfloat16)
            coarse = mass.astype(jnp.bfloat16).astype(jnp.float32)
            parts = [
                pick_ref[picked] * jnp.tile(jnp.concatenate([part, part], axis=0).astype(jnp.bfloat16), (item // 2, 1))
                for part in (coarse, mass - coarse)
            ]
            spread_ref[...] = lax.dot_general(
                jnp.concatenate(parts, axis=1),
                jnp.concatenate([hot, hot], axis=1),
                (((1,), (1,)), ((), ())),
                preferred_element_type=jnp.float32,
            )

        def add(index, spread_ref):
            base = list_ref[index] * item
            for first in range(0, item, ACCS):
                places = [rows_ref[base + first + k] for k in range(ACCS)]
                held = [acc[place] for acc, place in zip(accs, places)]
                for k in range(ACCS):
                    accs[k][places[k]] = held[k] + spread_ref[(first + k) * 8 : (first + k + 1) * 8, :]

        spread(0, even_ref)

        def pair(index, carry):
            spread(2 * index + 1, odd_ref)
            add(2 * index, even_ref)
            spread(2 * index + 2, even_ref)
            add(2 * index + 1, odd_ref)
            return carry

        lax.fori_loop(0, (active + 1) // 2, pair, 0)

    @pl.when(step > 0)
    def merge():
        flat = [acc.reshape((rows + 8) * 8, LANES) for acc in accs]
        base = (step - 1) * lats * lon_blocks * 8
        for lat in range(0, lats, 8):
            for lon in range(lon_blocks):
                at = pl.ds(lon * LANES, LANES)
                for b in range(bins):
                    picked = pl.ds(base + (lat * lon_blocks + lon) * 8 + b, 8, stride=lon_blocks * 8)
                    total = flat[0][picked, :]
                    for acc in flat[1:]:
                        total = total + acc[picked, :]
                    if with_field:
                        total = total + field_ref[0, b, pl.ds(lat, 8), at]
                    out_ref[0, b, pl.ds(lat, 8), at] = total


def deposit(field, shape, slots, cell_rows, counts, item, name):
    levels, bins, lats, lons = shape
    rows = levels * lats * lons // LANES
    per = lats // MERGE_ROWS

    def at(step):
        block = jnp.maximum(step - 1, 0)
        return (block // per, 0, block % per, 0)

    spec = pl.BlockSpec((1, bins, MERGE_ROWS, lons), at)
    fields = [] if field is None else [field]
    return pl.pallas_call(
        functools.partial(deposit_kernel, bool(fields), item),
        out_shape=jax.ShapeDtypeStruct(shape, jnp.float32),
        grid=(1 + levels * per,),
        in_specs=[SMEM, SMEM, VMEM] + [spec] * len(fields),
        out_specs=spec,
        scratch_shapes=[
            pltpu.SMEM((cell_rows.shape[0] // item + 8,), jnp.int32),
            pltpu.VMEM((8 * LANES, LANES), jnp.bfloat16),
            pltpu.VMEM((8 * item, LANES), jnp.float32),
            pltpu.VMEM((8 * item, LANES), jnp.float32),
        ]
        + [pltpu.VMEM((rows + 8, 8, LANES), jnp.float32)] * ACCS,
        compiler_params=BIG,
        cost_estimate=cost(22 if fields else 12),
        name=name,
    )(cell_rows, counts, slots, *fields)


def advance_kernel(
    first_bin, par_ref, f_ref, rim_ref, drop_ref, halo_ref, c_ref, ch_ref, cn_ref, adv_ref, hl_ref, p0, p1, keep_ref
):
    step = pl.program_id(0)
    unused, bins, lats, lons = f_ref.shape

    @pl.when(step == 0)
    def halo():
        def one(b, carry):
            above = halo_ref[0, b]
            for level in range(2):
                f = halo_ref[1 + level, b]
                rolled = pltpu.roll(f, 1, 0)
                p0[level, b] = rolled
                new = (
                    f
                    - ch_ref[0, level] * (f - pltpu.roll(f, 1, 1))
                    - ch_ref[1, level] * (f - rolled)
                    - ch_ref[2, level] * (f - above)
                )
                p1[level, b] = pltpu.roll(new, 1, 0)
                above = f
            return carry

        lax.fori_loop(0, bins, one, 0)

    @pl.when(step > 0)
    def main():
        top_row = lax.broadcasted_iota(jnp.int32, (8, lons), 0) == 0

        def south(prev, level, b, f):
            rolled = pltpu.roll(f, 1, 0)
            out = jnp.where(top_row, prev[level, b], rolled)
            prev[level, b] = rolled
            return out

        for lat in range(lats // 8):
            at = pl.ds(lat * 8, 8)

            keep = [1.0 - c_ref[0, level, at] - c_ref[1, level, at] - c_ref[2, level, at] for level in range(2)]
            for level in range(2):
                keep_ref[level] = keep[level]

            def flow(level, b, f, prev, above):
                new = (
                    keep_ref[level] * f
                    + c_ref[0, level, at] * pltpu.roll(f, 1, 1)
                    + c_ref[1, level, at] * south(prev, level, b, f)
                )
                return new if above is None else new + c_ref[2, level, at] * above

            def one(b, carry):
                scale = first_bin + b
                f0 = f_ref[0, b, at]
                f1 = f_ref[1, b, at]
                g0 = flow(0, b, f0, p0, rim_ref[b, at] + drop_ref[b, at])
                g1 = flow(1, b, f1, p0, f0)
                a0 = flow(0, b, g0, p1, None)
                a1 = flow(1, b, g1, p1, g0)
                adv_ref[0, b, at] = a0
                adv_ref[1, b, at] = a1
                low = (a1 + par_ref[scale] * (a0 * par_ref[8 + scale])) * par_ref[24 + scale]
                hl_ref[lat, b] = cn_ref[at] * g1 + par_ref[16 + scale] * low
                return carry

            lax.fori_loop(0, bins, one, 0)


def advance(half, params, field, rim, drop, halo, courant, courant_halo, courant_next):
    levels, all_bins, lats, lons = field.shape
    bins = all_bins // HALVES
    at = lambda step: jnp.maximum(step - 1, 0)
    return pl.pallas_call(
        functools.partial(advance_kernel, half * bins),
        out_shape=(
            jax.ShapeDtypeStruct((levels, bins, lats, lons), jnp.float32),
            jax.ShapeDtypeStruct((lats // 8, bins, 8, lons), jnp.float32),
        ),
        grid=(lats // ROWS + 1,),
        in_specs=[
            SMEM,
            pl.BlockSpec((levels, bins, ROWS, lons), lambda step: (0, half, at(step), 0)),
            pl.BlockSpec((bins, ROWS, lons), lambda step: (0, at(step), 0)),
            pl.BlockSpec((bins, ROWS, lons), lambda step: (half, at(step), 0)),
            pl.BlockSpec((3, bins, 8, lons), lambda step: (0, 0, 0, 0)),
            pl.BlockSpec((3, levels, ROWS, lons), lambda step: (0, 0, at(step), 0)),
            pl.BlockSpec((3, levels, 8, lons), lambda step: (0, 0, 0, 0)),
            pl.BlockSpec((ROWS, lons), lambda step: (at(step), 0)),
        ],
        out_specs=(
            pl.BlockSpec((levels, bins, ROWS, lons), lambda step: (0, 0, at(step), 0)),
            pl.BlockSpec((ROWS // 8, bins, 8, lons), lambda step: (at(step), 0, 0, 0)),
        ),
        scratch_shapes=[pltpu.VMEM((levels, bins, 8, lons), jnp.float32)] * 2 + [pltpu.VMEM((levels, 8, lons), jnp.float32)],
        compiler_params=BIG,
        cost_estimate=cost(9),
        name="advance",
    )(params, field, rim, drop, halo, courant, courant_halo, courant_next)


def cube_end_kernel(lam_ref, hl_ref, out_ref):
    count, bins = hl_ref.shape[:2]

    def one(b, carry):
        h = hl_ref[0, b]
        for member in range(1, count):
            h = hl_ref[member, b] + lam_ref[member * bins + b] * h
        out_ref[b] = h
        return carry

    lax.fori_loop(0, bins, one, 0)


def cube_scan_kernel(lam_ref, hl_ref, hin_ref, out_ref):
    count, bins = hl_ref.shape[:2]

    def one(b, carry):
        h = hin_ref[b]
        out_ref[0, b] = h
        for member in range(count - 1):
            h = hl_ref[member, b] + lam_ref[member * bins + b] * h
            out_ref[member + 1, b] = h
        return carry

    lax.fori_loop(0, bins, one, 0)


def finish_kernel(par_ref, mix_ref, *refs):
    *ins, out_ref = refs
    adv_refs, h_refs = ins[:HALVES], ins[HALVES:]
    unused, bins, lats, lons = out_ref.shape
    per = bins // HALVES
    tiles = range(lats // 8)

    def part(index, carry):
        at = pl.ds(pl.multiple_of(index * LANES, LANES), LANES)
        above = [jnp.concatenate([h_refs[b // per][t, b % per, :, at] for t in tiles], axis=1) for b in range(bins)]
        for level in range(2):
            solved = []
            for b in range(bins):
                adv = [adv_refs[b // per][level, b % per, t * 8 : t * 8 + 8, at] for t in tiles]
                s = (jnp.concatenate(adv, axis=1) + above[b]) * par_ref[16 * level + 8 + b]
                solved.append(s)
                above[b] = par_ref[b] * s
            whole = jnp.concatenate(solved, axis=0)
            coarse = whole.astype(jnp.bfloat16)
            fine = (whole - coarse.astype(jnp.float32)).astype(jnp.bfloat16)
            mixed = jnp.dot(
                mix_ref[...], jnp.concatenate([coarse, coarse, fine], axis=0), preferred_element_type=jnp.float32
            )
            for i in range(bins):
                total = solved[i]
                for j in range(bins):
                    row = 8 * (bins + i * bins + j)
                    total = total + mixed[row : row + 8] * solved[j]
                total = total / (1.0 + mixed[8 * i : 8 * i + 8])
                for t in tiles:
                    out_ref[level, i, t * 8 : t * 8 + 8, at] = total[:, t * LANES : (t + 1) * LANES]
        return carry

    lax.fori_loop(0, lons // LANES, part, 0, unroll=True)


def mixing(coag_loss, coag_gain):
    bins = coag_loss.shape[0]
    both = jnp.concatenate([coag_loss, coag_gain.reshape(bins * bins, bins)], axis=0)
    eye = jnp.eye(8, dtype=jnp.float32)
    matrix = (both[:, None, :, None] * eye[None, :, None, :]).reshape(both.shape[0] * 8, bins * 8)
    coarse = matrix.astype(jnp.bfloat16)
    fine = (matrix - coarse.astype(jnp.float32)).astype(jnp.bfloat16)
    return jnp.concatenate([coarse, fine, coarse], axis=1)


def finish(params, mix, adv, h):
    levels, per, lats, lons = adv[0].shape
    bins = per * HALVES
    rows = ROWS // 2
    return pl.pallas_call(
        finish_kernel,
        out_shape=jax.ShapeDtypeStruct((levels, bins, lats, lons), jnp.float32),
        grid=(lats // rows,),
        in_specs=[SMEM, VMEM]
        + [pl.BlockSpec((levels, per, rows, lons), lambda step: (0, 0, step, 0))] * HALVES
        + [pl.BlockSpec((rows // 8, per, 8, lons), lambda step: (step, 0, 0, 0))] * HALVES,
        out_specs=pl.BlockSpec((levels, bins, rows, lons), lambda step: (0, 0, step, 0)),
        compiler_params=BIG,
        cost_estimate=cost(10),
        name="finish",
    )(params, mix, *adv, *h)


def shifted(value, axis, steps):
    count = lax.axis_size(axis)
    first, last = (max(0, -steps), min(count, count - steps))
    return lax.ppermute(value, axis, [(source, source + steps) for source in range(first, last)])


def on_device(field, courant, parcel_mass, parcel_owner, parcel_cell, settle, coag_gain, coag_loss):
    levels, bins, lats, lons = field.shape
    n_lev = lax.axis_size("lev")
    devices = lax.axis_size(("lat", "lev"))
    cube = lats // 8
    cubes = n_lev // cube
    here = lax.axis_index("lev")

    per = bins // HALVES
    early_rim = shifted(field[-1, :per], "lev", 1)
    slots = route(parcel_mass, parcel_owner, parcel_cell, devices, lats * lons)
    slots, courant = lax.optimization_barrier((slots, courant))
    courant_next = shifted(courant[2, 0], "lev", -1)
    courant_halo = shifted(courant[:, :, -8:], "lat", 1)
    slots = lax.all_to_all(slots, ("lat", "lev"), split_axis=0, concat_axis=0, tiled=True)
    cap_lanes = slots.shape[2] - LANES
    blocks = cap_lanes // LANES
    level_rows = lats * lons // LANES
    rim_slots = shifted(slots, "lev", 1)

    def tables(slots, row):
        codes = slots[:, :blocks, cap_lanes:].astype(jnp.int32).reshape(devices * cap_lanes)
        counts = slots[:, row, cap_lanes].astype(jnp.int32)
        return codes // LANES, counts

    rows, counts = tables(slots, blocks)
    f0 = deposit(field, field.shape, slots, rows, counts, LANES, "deposit")
    rim_slots, later_rim = lax.optimization_barrier((rim_slots, field[-1, per:]))
    raw_rims = [early_rim, shifted(later_rim, "lev", 1)]
    rows, counts = tables(rim_slots, blocks + 1)
    rows = jnp.where(rows < level_rows, level_rows, rows - level_rows)
    drop = deposit(None, (1,) + field.shape[1:], rim_slots, rows, counts, LANES // 2, "deposit_rim")[0]
    pairs = settle.reshape(bins, n_lev, 2)
    first, second = pairs[:, :, 0], pairs[:, :, 1]
    table = jnp.stack([first, 1.0 / (1.0 + first), second, 1.0 / (1.0 + second)], axis=0)
    params = lax.dynamic_index_in_dim(table, here, axis=2, keepdims=False).reshape(4 * bins)
    lam = (table[0] * table[1] * table[2] * table[3]).T
    lam = lax.dynamic_slice_in_dim(lam, here // cube * cube, cube, axis=0)
    mix = mixing(coag_loss, coag_gain)

    groups = [list(range(c * cube, (c + 1) * cube)) for c in range(cubes)]
    swap = functools.partial(
        lax.all_to_all, axis_name="lev", split_axis=0, concat_axis=0, axis_index_groups=groups, tiled=True
    )
    advs, hs = [], []
    for half in range(HALVES):
        own = slice(half * per, (half + 1) * per)
        raw_rim = raw_rims[half]
        if half:
            advs[-1], raw_rim = lax.optimization_barrier((advs[-1], raw_rim))
        rim_halo = raw_rim[:, -8:] + drop[own, -8:]
        halo = shifted(jnp.concatenate([rim_halo[None], f0[:, own, -8:]], axis=0), "lat", 1)
        adv, hl = advance(half, params, f0, raw_rim, drop, halo, courant, courant_halo, courant_next)
        advs.append(adv)
        hs.append(swap(hl))
    for half in range(HALVES):
        hs[half] = swap(carry_scan(hs[half], lam[:, half * per : (half + 1) * per], cubes))
    return finish(params, mix, advs, hs)


def carry_scan(hl, lam, cubes):
    cube = hl.shape[0]
    flat_lam = lam.reshape(-1)
    end = pl.pallas_call(
        cube_end_kernel,
        out_shape=jax.ShapeDtypeStruct(hl.shape[1:], jnp.float32),
        in_specs=[SMEM, VMEM],
        out_specs=VMEM,
        compiler_params=BIG,
        cost_estimate=cost(2),
        name="cube_end",
    )(flat_lam, hl)
    reach = 1
    factor = jnp.prod(lam, axis=0)[:, None, None]
    while reach < cubes - 1:
        end = end + factor * shifted(end, "lev", reach * cube)
        factor = factor * shifted(factor, "lev", reach * cube)
        reach = 2 * reach
    carried = shifted(end, "lev", cube)
    return pl.pallas_call(
        cube_scan_kernel,
        out_shape=jax.ShapeDtypeStruct(hl.shape, jnp.float32),
        in_specs=[SMEM, VMEM, VMEM],
        out_specs=VMEM,
        compiler_params=BIG,
        cost_estimate=cost(2),
        name="cube_scan",
    )(flat_lam, hl, carried)


def solution(mesh):
    in_specs = (
        P("lev", None, "lat", None),
        P(None, "lev", "lat", None),
        P(None, ("lat", "lev")),
        P(("lat", "lev"), None),
        P(("lat", "lev")),
        P(),
        P(),
        P(),
    )
    out_specs = P("lev", None, "lat", None)
    return jax.shard_map(
        on_device, mesh=mesh, in_specs=in_specs, out_specs=out_specs, check_vma=False
    )
```
